32 devices in a mesh: dp: 2 (over x), gx: 16 (over z, y, core).
Axes of the slice: x: 2, y: 2, z: 4, core: 2. Of those that a mesh axis runs over, the one named last changes fastest.
Arguments:
- field: bfloat16 [2, 16, 32, 128, 128], P('dp', 'gx'), may hold values from -6 to 6
- cotangent: bfloat16 [2, 16, 32, 128, 128], P('dp', 'gx'), may hold values from -6 to 6
- spectral_weight: bfloat16 [512, 16, 2048], P('gx'), may hold values from -3 to 3
- pointwise_weight: bfloat16 [32, 32], replicated, may hold values from -1 to 1
Outputs:
- field_grad: bfloat16 [2, 16, 32, 128, 128], P('dp', 'gx')
- weight_grad: float32 [512, 16, 2048], P('gx', 'dp')
The draws below stay inside these ranges and needn't reach their ends.
All inputs are finite; a program needn't handle non-finite values.
Results may differ from the reference program's by a relative error of at most 0.001.
Values sent between devices are 32-bit elements; how exact they have to be, the bound alone decides.
No kernel may reach another device: no remote copies, remote signals or barrier semaphores. Data moves between devices by JAX's collectives and lax.ppermute only.
A program may use at most 64 MiB of HBM per device.

```python
import jax
import jax.numpy as jnp
from jax import lax

C = 32
M = 16
NY = 128
NZ = 128
NX = 16
MX = 8
KX = 16
PAIRS = 512
SAMPLES = 2


def level_of(stream_key, extent, cuts, low, high):
    level, own = 1.0, jax.random.fold_in(stream_key, 6)
    for dim, parts in cuts:
        draws = jnp.exp(jax.random.uniform(jax.random.fold_in(own, dim), (parts,), jnp.float32, low / len(cuts), high / len(cuts)))
        level = level * jnp.repeat(draws, extent[dim] // parts).reshape([-1 if axis == dim else 1 for axis in range(len(extent))])
    return level


def bell_draw(key, dims, spread, bound, pieces=(), kind=jnp.bfloat16):
    result = jax.random.normal(key, dims, jnp.float32) * spread
    if len(pieces) > 0:
        result = level_of(key, dims, pieces, -0.22, 0.18) * result
    return jnp.clip(result, min=-bound, max=bound).astype(kind)


def setup_inputs(seed: int = 0) -> dict:
    seeds = jax.random.split(jax.random.key(seed), 5)
    field = bell_draw(seeds[0], (SAMPLES, NX, C, NY, NZ), 1.0, 6.0, ((0, 2), (1, 16)))
    cotangent = bell_draw(seeds[1], (SAMPLES, NX, C, NY, NZ), 1.0, 6.0, ((0, 2), (1, 16)))
    spectral_weight = bell_draw(seeds[2], (PAIRS, KX, 2 * C * C), 0.5, 3.0, ((0, 16),))
    pointwise_weight = bell_draw(seeds[3], (C, C), C ** -0.5, 1.0)
    return dict(field=field, cotangent=cotangent, spectral_weight=spectral_weight, pointwise_weight=pointwise_weight)


def kept_freqs(half_count, length):
    index_range = jnp.arange(2 * half_count, dtype=jnp.int32)
    return jnp.where(index_range < half_count, index_range, index_range + length - 2 * half_count).astype(jnp.int32)

def spectral(values, real_w, imag_w):
    freq_x = kept_freqs(MX, NX)
    freq_y = kept_freqs(M, NY)
    transform = jnp.fft.rfftn(values, axes=(0, 2, 3))
    picked = transform[freq_x][:, :, freq_y][:, :, :, :M]
    flattened = picked.reshape(KX, C, PAIRS)
    weight = lax.complex(real_w, imag_w)
    mixed = jnp.einsum('kiq,qkio->koq', flattened, weight)
    mode_block = mixed.reshape(KX, C, 2 * M, M)
    padded_rows = jnp.zeros((KX, C, NY, NZ // 2 + 1), transform.dtype).at[:, :, freq_y, :M].set(mode_block)
    spectrum = jnp.zeros((NX, C, NY, NZ // 2 + 1), transform.dtype).at[freq_x].set(padded_rows)
    return jnp.fft.irfftn(spectrum, s=(NX, NY, NZ), axes=(0, 2, 3))

def reference(field, cotangent, spectral_weight, pointwise_weight):
    weight = spectral_weight.astype(jnp.float32).reshape(PAIRS, KX, 2, C, C)
    real_w = weight[:, :, 0]
    imag_w = weight[:, :, 1]
    pointwise = pointwise_weight.astype(jnp.float32)
    field_grads = []
    total_real = jnp.zeros((PAIRS, KX, C, C), jnp.float32)
    total_imag = jnp.zeros((PAIRS, KX, C, C), jnp.float32)
    for sample in range(SAMPLES):
        values = field[sample].astype(jnp.float32)
        upstream = cotangent[sample].astype(jnp.float32)
        output_unused, pullback = jax.vjp(spectral, values, real_w, imag_w)
        d_values, d_real, d_imag = pullback(upstream)
        linear = jnp.einsum('pdyz,cd->pcyz', upstream, pointwise)
        field_grads.append((d_values + linear).astype(jnp.bfloat16))
        total_real = total_real + d_real
        total_imag = total_imag + d_imag
    weight_grad = jnp.stack([total_real, total_imag], axis=2).reshape(PAIRS, KX, 2 * C * C)
    return (jnp.stack(field_grads), weight_grad)
```

```python
import math

import jax
import jax.numpy as jnp
import ml_dtypes
import numpy as np
from jax import lax
from jax.experimental import pallas as pl
from jax.experimental.pallas import tpu as pltpu
from jax.sharding import PartitionSpec as P

M = 16
F32 = jnp.float32
BF16 = jnp.bfloat16
VMEM_LIMIT = 56 * 1024 * 1024


def kept_freqs(half_count, length):
    index = np.arange(2 * half_count)
    return np.where(index < half_count, index, index + length - 2 * half_count)


def phases(frequency, length):
    product = np.outer(frequency, np.arange(length)) % length
    angle = product * (2.0 * math.pi / length)
    return np.cos(angle), np.sin(angle)


def split_np(table):
    high = table.astype(ml_dtypes.bfloat16)
    low = (table - high.astype(np.float64)).astype(ml_dtypes.bfloat16)
    return high, low


def split(value):
    high = value.astype(BF16)
    low = (value - high.astype(F32)).astype(BF16)
    return high, low


def dot(left, right):
    return jnp.dot(left, right, preferred_element_type=F32)


def forward_tables(length_y, length_z):
    cos_y, sin_y = phases(kept_freqs(M, length_y), length_y)
    high, low = split_np(np.concatenate([cos_y, -sin_y], 0))
    along_y = np.concatenate([high, low], 0)
    cos_z, sin_z = phases(np.arange(M), length_z)
    block = np.zeros((2, length_z, 2, M))
    block[0, :, 0], block[1, :, 0] = cos_z.T, sin_z.T
    block[0, :, 1], block[1, :, 1] = -sin_z.T, cos_z.T
    along_z = np.zeros((8, 2, length_z, 2, 8, M))
    for place in range(8):
        along_z[place, :, :, :, place, :] = block
    along_z = along_z.reshape(8, 2 * length_z, 2 * 8 * M)
    return along_y, np.stack(split_np(along_z))


def inverse_tables(length_y, length_z):
    cos_z, sin_z = phases(np.arange(M), length_z)
    along_z = np.zeros((2, 8, M, 8, 2, length_z))
    for place in range(8):
        along_z[0, place, :, place, 0] = cos_z
        along_z[1, place, :, place, 0] = -sin_z
        along_z[0, place, :, place, 1] = sin_z
        along_z[1, place, :, place, 1] = cos_z
    along_z = along_z.reshape(2 * 8 * M, 8 * 2 * length_z)
    cos_y, sin_y = phases(kept_freqs(M, length_y), length_y)
    high, low = split_np(np.concatenate([cos_y.T, -sin_y.T], 1))
    return np.stack(split_np(along_z)), np.concatenate([high, high, low], 1)


def x_tables(kept_x, width_x):
    cos_x, sin_x = phases(kept_freqs(kept_x // 2, width_x), width_x)
    high, low = split_np(np.concatenate([cos_x, sin_x], 1))
    forward = np.concatenate([high, high, low], 1)
    high, low = split_np(np.concatenate([cos_x.T, sin_x.T], 1))
    inverse = np.concatenate([high, high, low], 1)
    return forward, inverse


def spread_table(channels):
    copies = 128 // channels
    table = np.zeros((2, 2, 2, channels, 2, copies, channels))
    eye = np.eye(channels)
    for part in range(2):
        table[:, part, 1, :, part] = eye[:, None, :]
    return table.reshape(8 * channels, 256).astype(ml_dtypes.bfloat16)


def gather_table(channels):
    table = np.zeros((2, channels, channels, 2, 2, 2, channels))
    for i in range(channels):
        table[0, i, :, 0, :, 0, i] = 1.0
        table[1, i, :, 0, :, 1, i] = 1.0
        table[1, i, :, 1, :, 0, i] = -1.0
        table[0, i, :, 1, :, 1, i] = 1.0
    return table.reshape(2 * channels * channels, 8 * channels).astype(ml_dtypes.bfloat16)


def repeat_table(channels):
    square = channels * channels
    table = np.zeros((2, 2, 2, channels, 2 * square + 256))
    for i in range(channels):
        for part in range(2):
            start = part * square + i * channels
            table[:, part, 0, i, start : start + channels] = 1.0
            table[:, part, 1, i, 2 * square + part * 128 + i : 2 * square + part * 128 + 128 : channels] = 1.0
    return table.reshape(8 * channels, -1).astype(ml_dtypes.bfloat16)


def forward_kernel(scale_ref, field_ref, cot_ref, fy_ref, fz_ref, out_ref, rows_ref):
    channels, length_y, length_z = field_ref.shape
    kept = 4 * M
    for array, ref in enumerate((field_ref, cot_ref)):
        for pair in range(channels // 2):
            data = jnp.concatenate([ref[2 * pair], ref[2 * pair + 1]], axis=1)
            both = dot(fy_ref[...], data)
            value = both[:kept] + both[kept:]
            start = (array * channels + 2 * pair) * kept
            rows_ref[start : start + kept, :] = value[:, :length_z]
            rows_ref[start + kept : start + 2 * kept, :] = value[:, length_z:]
    count = 2 * channels
    total = None
    for place in range(8):
        pieces = []
        for group in range(2 * M // 8):
            ky = group * 8 + place
            real = rows_ref[pl.ds(ky, count, stride=kept), :]
            imag = rows_ref[pl.ds(2 * M + ky, count, stride=kept), :]
            pieces.append(jnp.concatenate([real, imag], axis=1))
        high, low = split(jnp.concatenate(pieces, axis=0))
        size = high.shape[0]
        both = dot(jnp.concatenate([high, low], axis=0), fz_ref[0, place])
        term = both[:size] + both[size:] + dot(high, fz_ref[1, place])
        total = term if total is None else total + term
    for group in range(2 * M // 8):
        block = total[group * count : (group + 1) * count] * scale_ref[...]
        stacked = jnp.concatenate([block[:, :128], block[:, 128:]], axis=0)
        out_ref[group * 128 : (group + 1) * 128, :] = stacked.T


def mid_kernel(
    planes_ref, weight_ref, fx_ref, ix_ref, spread_ref, gather_ref,
    modes_ref, out_ref, rows_ref, high_ref, low_ref,
):
    pairs, kept_x, _ = weight_ref.shape
    width_x = planes_ref.shape[0] // pairs
    pack = width_x * pairs // out_ref.shape[0]
    halves, _, share, lanes = modes_ref.shape
    lane = lax.broadcasted_iota(jnp.int32, (width_x, 128), 1)
    sign = jnp.where(lane < 64, 1.0, -1.0).astype(F32)
    for step in range(pairs // 2):
        columns = []
        for q in (2 * step, 2 * step + 1):
            plane = planes_ref[pl.ds(q, width_x, stride=pairs), :]
            turned = pltpu.roll(plane, 64, 1) * sign
            columns.append(jnp.concatenate([plane, turned], axis=0))
        high, low = split(jnp.concatenate(columns, axis=1))
        modes = dot(fx_ref[...], jnp.concatenate([high, low, high], axis=0))
        for index, q in enumerate((2 * step, 2 * step + 1)):
            mode = modes[:, index * 128 : (index + 1) * 128]
            rows_ref[q * kept_x : (q + 1) * kept_x, :] = mode
            for half in range(halves):
                modes_ref[half, q] = mode[half * share : (half + 1) * share]
    square = weight_ref.shape[2] // 2
    for q in range(pairs):
        high, low = split(rows_ref[q * kept_x : (q + 1) * kept_x, :])
        spread = dot(jnp.concatenate([high, low], axis=1), spread_ref[...])
        real, imag = spread[:, :128], spread[:, 128:]
        rows = pl.ds(q * kept_x, kept_x)
        for start in range(0, square, 128):
            w_real = weight_ref[q, :, start : start + 128].astype(F32)
            w_imag = weight_ref[q, :, square + start : square + start + 128].astype(F32)
            first = split(real * w_real + imag * w_imag)
            second = split(imag * w_real - real * w_imag)
            high_ref[rows, start : start + 128] = first[0]
            low_ref[rows, start : start + 128] = first[1]
            high_ref[rows, square + start : square + start + 128] = second[0]
            low_ref[rows, square + start : square + start + 128] = second[1]
    grads = dot(high_ref[...], gather_ref[...]) + dot(low_ref[...], gather_ref[...])
    count = pairs // pack
    if pack == 2:
        size = count * kept_x
        lane = lax.broadcasted_iota(jnp.int32, (size, 256), 1) % 128
        grads = jnp.where(lane < 64, grads[:size], grads[size:])
    for step in range(count // 2):
        columns = []
        for row in (2 * step, 2 * step + 1):
            block = grads[row * kept_x : (row + 1) * kept_x]
            columns.append(jnp.concatenate([block[:, :128], block[:, 128:]], axis=0))
        high, low = split(jnp.concatenate(columns, axis=1))
        planes = dot(ix_ref[...], jnp.concatenate([high, low, high], axis=0))
        for index, row in enumerate((2 * step, 2 * step + 1)):
            out_ref[pl.ds(row, width_x, stride=count), :] = planes[:, index * 128 : (index + 1) * 128]


def weight_kernel(mine_ref, other_ref, repeat_ref, out_ref):
    pairs, share, _ = mine_ref.shape
    square = out_ref.shape[2] // 2
    chunk = min(pairs, 8)

    @pl.loop(0, pairs // chunk)
    def _(step):
        base = step * chunk
        sides = []
        for ref in (mine_ref, other_ref):
            rows = ref[pl.ds(base, chunk)].reshape(chunk * share, 128)
            high, low = split(rows)
            sides.append(jnp.concatenate([high, low], axis=1))
        spread = [dot(side, repeat_ref[:, 2 * square :]) for side in sides]
        for start in range(0, square, 256):
            real = imag = None
            for side, cots in zip(sides, spread):
                f_real = dot(side, repeat_ref[:, start : start + 256])
                f_imag = dot(side, repeat_ref[:, square + start : square + start + 256])
                c_real = jnp.concatenate([cots[:, :128]] * 2, axis=1)
                c_imag = jnp.concatenate([cots[:, 128:]] * 2, axis=1)
                one = f_real * c_real + f_imag * c_imag
                two = f_real * c_imag - f_imag * c_real
                real = one if real is None else real + one
                imag = two if imag is None else imag + two
            out_ref[pl.ds(base, chunk), :, start : start + 256] = real.reshape(chunk, share, 256)
            out_ref[pl.ds(base, chunk), :, square + start : square + start + 256] = imag.reshape(
                chunk, share, 256
            )


def inverse_kernel(planes_ref, cot_ref, mix_ref, iz_ref, iy_ref, out_ref, rows_ref, linear_ref):
    channels, length_y, length_z = cot_ref.shape
    rows, _ = planes_ref.shape
    pack = 2 * M * M // rows
    kept = 4 * M
    pieces = []
    order = []
    for block in range(rows // 128):
        turned = planes_ref[block * 128 : (block + 1) * 128, :].T
        for low_bit in range(pack):
            start = low_bit * 2 * channels
            pieces.append(
                jnp.concatenate(
                    [turned[start : start + channels], turned[start + channels : start + 2 * channels]], axis=1
                )
            )
            order.append((block, low_bit))
    high, low = split(jnp.concatenate(pieces, axis=0))
    size = high.shape[0]
    both_terms = jnp.concatenate([high, low], axis=0)
    for place in range(8):
        for part in range(2):
            column = (place * 2 + part) * length_z
            both = dot(both_terms, iz_ref[0, :, column : column + length_z])
            value = both[:size] + both[size:] + dot(high, iz_ref[1, :, column : column + length_z])
            for index, (block, low_bit) in enumerate(order):
                ky = (block * 8 + place) * pack + low_bit
                start = (part * 2 * M + ky) * channels
                rows_ref[start : start + channels, :] = value[index * channels : (index + 1) * channels]
    for step in range(length_y // 32):
        columns = []
        for part in range(2):
            first = step * 32 + part * 16
            columns.append(cot_ref[:, first : first + 16, :].reshape(channels * 16, length_z))
        mixed = dot(mix_ref[...], jnp.concatenate(columns, axis=1))
        for part in range(2):
            first = step * 32 + part * 16
            linear_ref[:, first : first + 16, :] = mixed[:, part * length_z : (part + 1) * length_z].reshape(
                channels, 16, length_z
            )
    for pair in range(channels // 2):
        columns = [rows_ref[pl.ds(2 * pair + side, kept, stride=channels), :] for side in range(2)]
        high, low = split(jnp.concatenate(columns, axis=1))
        value = dot(iy_ref[...], jnp.concatenate([high, low, high], axis=0))
        for side in range(2):
            channel = 2 * pair + side
            spectral = value[:, side * length_z : (side + 1) * length_z]
            out_ref[channel] = (spectral + linear_ref[channel]).astype(BF16)


def call(kernel, out_shape, scratch, flops, moved, *args):
    return pl.pallas_call(
        kernel,
        out_shape=out_shape,
        scratch_shapes=scratch,
        compiler_params=pltpu.CompilerParams(vmem_limit_bytes=VMEM_LIMIT),
        cost_estimate=pl.CostEstimate(flops=flops, bytes_accessed=moved, transcendentals=0),
    )(*args)


def weight_terms(modes, channels):
    parts = modes.reshape(modes.shape[:3] + (2, 2, channels))
    in_real, in_imag = parts[..., 0, 0, :, None], parts[..., 1, 0, :, None]
    cot_real, cot_imag = parts[..., 0, 1, None, :], parts[..., 1, 1, None, :]
    real = jnp.sum(in_real * cot_real + in_imag * cot_imag, axis=0)
    imag = jnp.sum(in_real * cot_imag - in_imag * cot_real, axis=0)
    stacked = jnp.stack([real, imag], axis=2)
    return stacked.reshape(stacked.shape[:2] + (-1,))


def on_device(field, cotangent, spectral_weight, pointwise_weight):
    _, planes, channels, length_y, length_z = field.shape
    pairs, kept_x, _ = spectral_weight.shape
    groups = lax.axis_size("gx")
    samples = lax.axis_size("dp")
    width_x = planes * groups
    share = kept_x // samples
    pack = 2 if pairs == 2 * M else 1
    count = pairs // pack
    all_pairs = 2 * M * M
    cells = width_x * length_y * length_z
    shape = jax.ShapeDtypeStruct
    field = field.reshape(channels, length_y, length_z)
    cotangent = cotangent.reshape(channels, length_y, length_z)

    fy, fz = forward_tables(length_y, length_z)
    iz, iy = inverse_tables(length_y, length_z)
    fx, ix = x_tables(kept_x, width_x)
    scale = np.ones((2, channels, 2, 8, M), np.float32)
    scale[1] = np.where(np.arange(M) == 0, 1.0, 2.0) / cells
    scale = scale.reshape(2 * channels, 256)

    spectra = call(
        forward_kernel,
        shape((all_pairs, 128), F32),
        [pltpu.VMEM((2 * channels * 4 * M, length_z), F32)],
        10**9, 5 * 10**6,
        scale, field, cotangent, fy, fz,
    )
    received = lax.all_to_all(
        spectra.reshape(groups, pairs, 128), "gx", split_axis=0, concat_axis=0, tiled=True
    )
    modes, grads = call(
        mid_kernel,
        (shape((samples, pairs, share, 128), F32), shape((width_x * count, 128), F32)),
        [
            pltpu.VMEM((pairs * kept_x, 128), F32),
            pltpu.VMEM((pairs * kept_x, 2 * channels * channels), BF16),
            pltpu.VMEM((pairs * kept_x, 2 * channels * channels), BF16),
        ],
        10**9, 4 * 10**6,
        received.reshape(width_x * pairs, 128), spectral_weight, fx, ix,
        spread_table(channels), gather_table(channels),
    )
    returned = lax.all_to_all(
        grads.reshape(groups, count, 128), "gx", split_axis=0, concat_axis=0, tiled=True
    )
    if samples == 2 and share % 8 == 0:
        me = lax.axis_index("dp")
        mine = lax.dynamic_index_in_dim(modes, me, 0, keepdims=False)
        other = lax.dynamic_index_in_dim(modes, 1 - me, 0, keepdims=False)
        other = lax.ppermute(other, "dp", [(0, 1), (1, 0)])
        weight_grad = call(
            weight_kernel,
            shape((pairs, share, 2 * channels * channels), F32),
            [],
            10**9, 3 * 10**6,
            mine, other, repeat_table(channels),
        )
    else:
        modes = lax.all_to_all(modes, "dp", split_axis=0, concat_axis=0, tiled=True)
        weight_grad = weight_terms(modes, channels)

    eye = jnp.eye(16, dtype=BF16)
    mix = (pointwise_weight[:, None, :, None] * eye[None, :, None, :]).reshape(16 * channels, 16 * channels)
    field_grad = call(
        inverse_kernel,
        shape((channels, length_y, length_z), BF16),
        [pltpu.VMEM((4 * M * channels, length_z), F32), pltpu.VMEM((channels, length_y, length_z), F32)],
        10**9, 4 * 10**6,
        returned.reshape(width_x * count, 128), cotangent, mix, iz, iy,
    )
    return field_grad.reshape(1, planes, channels, length_y, length_z), weight_grad


def solution(mesh):
    placed = (
        P("dp", "gx", None, None, None),
        P("dp", "gx", None, None, None),
        P("gx", None, None),
        P(),
    )
    return jax.shard_map(
        on_device,
        mesh=mesh,
        in_specs=placed,
        out_specs=(P("dp", "gx", None, None, None), P("gx", "dp", None)),
        check_vma=False,
    )
```

```python
import functools
import math

import jax
import jax.numpy as jnp
import ml_dtypes
import numpy as np
from jax import lax
from jax.experimental import pallas as pl
from jax.experimental.pallas import tpu as pltpu
from jax.sharding import PartitionSpec as P

M = 16
F32 = jnp.float32
BF16 = jnp.bfloat16
MIB = 1024 * 1024
ROWS = 3 * M


def kept_freqs(half_count, length):
    index = np.arange(2 * half_count)
    return np.where(index < half_count, index, index + length - 2 * half_count)


def phases(frequency, length):
    product = np.outer(frequency, np.arange(length)) % length
    angle = product * (2.0 * math.pi / length)
    return np.cos(angle), np.sin(angle)


def split_np(table):
    high = table.astype(ml_dtypes.bfloat16)
    low = (table - high.astype(np.float64)).astype(ml_dtypes.bfloat16)
    return high, low


def split(value):
    high = value.astype(BF16)
    low = (value - high.astype(F32)).astype(BF16)
    return high, low


def dot(left, right):
    return jnp.dot(left, right, preferred_element_type=F32)


def forward_tables(length_y, length_z):
    cos_y, sin_y = phases(np.arange(M + 1), length_y)
    rows = np.zeros((ROWS, length_y))
    rows[:M], rows[M : 2 * M] = cos_y[:M], -sin_y[:M]
    rows[2 * M], rows[2 * M + 1] = cos_y[M], -sin_y[M]
    along_y = np.concatenate(split_np(rows), 1)
    cos_z, sin_z = phases(np.arange(M), length_z)
    along_z = np.concatenate([np.tile(cos_z.T, (1, 8)), np.tile(sin_z.T, (1, 8))], 1)
    return along_y, np.stack(split_np(along_z))


def inverse_tables(length_y, length_z):
    cos_z, sin_z = phases(np.arange(M), length_z)
    along_z = np.zeros((2, 2, 8, M, 2, length_z))
    for place in range(8):
        along_z[0, 0, place, :, place % 2] = cos_z
        along_z[0, 1, place, :, place % 2] = -sin_z
        along_z[1, 0, place, :, place % 2] = sin_z
        along_z[1, 1, place, :, place % 2] = cos_z
    along_z = along_z.reshape(2, 2 * 8 * M, 2 * length_z)
    along_z = np.stack([np.stack(split_np(part)) for part in along_z])
    cos_y, sin_y = phases(np.arange(M + 1), length_y)
    columns = np.zeros((length_y, ROWS))
    for k in range(M + 1):
        columns[:, mode_row(0, k)] = cos_y[k]
        columns[:, mode_row(1, k)] = -sin_y[k]
    high, low = split_np(columns)
    return along_z, np.concatenate([high, high, low], 1)


def mode_row(part, k):
    return 2 * M + part if k == M else part * M + k


def x_tables(kept_x, width_x):
    cos_x, sin_x = phases(kept_freqs(kept_x // 2, width_x), width_x)
    high, low = split_np(np.concatenate([cos_x, sin_x], 1))
    forward = np.concatenate([high, high, low], 1)
    high, low = split_np(np.concatenate([cos_x.T, sin_x.T], 1))
    inverse = np.concatenate([high, high, low], 1)
    return forward, inverse


def spread_table(channels):
    copies = 128 // channels
    table = np.zeros((2, 2, 2, channels, 2, copies, channels))
    eye = np.eye(channels)
    for part in range(2):
        table[:, part, 1, :, part] = eye[:, None, :]
    return table.reshape(8 * channels, 256).astype(ml_dtypes.bfloat16)


def gather_table(channels):
    table = np.zeros((2, channels, channels, 2, 2, 2, channels))
    for i in range(channels):
        table[0, i, :, 0, :, 0, i] = 1.0
        table[1, i, :, 0, :, 1, i] = 1.0
        table[1, i, :, 1, :, 0, i] = -1.0
        table[0, i, :, 1, :, 1, i] = 1.0
    return table.reshape(2 * channels * channels, 8 * channels).astype(ml_dtypes.bfloat16)


def repeat_table(channels):
    square = channels * channels
    table = np.zeros((2, 2, channels, 2 * square + 256))
    for i in range(channels):
        for part in range(2):
            start = part * square + i * channels
            table[part, 0, i, start : start + channels] = 1.0
            table[part, 1, i, 2 * square + part * 128 + i : 2 * square + part * 128 + 128 : channels] = 1.0
    return table.reshape(4 * channels, -1).astype(ml_dtypes.bfloat16)


def forward_kernel(
    field_hbm, cot_hbm, scale_hbm, fy_hbm, fz_hbm,
    out_ref, data_ref, scale_ref, fy_ref, fz_ref, rows_ref, sems,
):
    channels, _, length_z = field_hbm.shape
    copies = []

    def start(source, target):
        copy = pltpu.make_async_copy(source, target, sems.at[len(copies)])
        copy.start()
        copies.append(copy)
        return copy

    half = channels // 2
    table_y = start(fy_hbm, fy_ref)
    chunks = []
    for array, ref in enumerate((field_hbm, cot_hbm)):
        for first in (0, half):
            part = pl.ds(first, half)
            chunks.append((array, first, start(ref.at[part], data_ref.at[array, part])))
        if array == 0:
            table_z = start(fz_hbm, fz_ref)
            table_scale = start(scale_hbm, scale_ref)
    table_y.wait()
    for array, first, copy in chunks:
        copy.wait()
        for pair in range(first // 2, (first + half) // 2):
            data = jnp.concatenate([data_ref[array, 2 * pair], data_ref[array, 2 * pair + 1]], axis=1)
            value = dot(fy_ref[...], jnp.concatenate([data, data], axis=0))
            base = (array * channels + 2 * pair) * ROWS
            rows_ref[base : base + ROWS, :] = value[:, :length_z]
            rows_ref[base + ROWS : base + 2 * ROWS, :] = value[:, length_z:]
    table_z.wait()
    table_scale.wait()
    count = 2 * channels
    group = lax.broadcasted_iota(jnp.int32, (16, 256), 1) // M % 8
    lefts, rights = [], []
    for place in range(8):
        keep = jnp.where(group == place, 1.0, 0.0).astype(BF16)
        keep = jnp.concatenate([keep] * (length_z // 16), axis=0)
        table_high, table_low = fz_ref[0] * keep, fz_ref[1] * keep
        sources = [part * M + octet * 8 + place for part in range(2) for octet in range(2)]
        if place == 0:
            sources += [2 * M, 2 * M + 1]
        rows = [rows_ref[pl.ds(source, count, stride=ROWS), :] for source in sources]
        high, low = split(jnp.concatenate(rows, axis=0))
        left = jnp.concatenate([high, low, high], axis=1)
        right = jnp.concatenate([table_high, table_high, table_low], axis=0)
        if place == 0:
            last = dot(left[4 * count :], right)
            left = left[: 4 * count]
        lefts.append(left)
        rights.append(right)
    total = dot(jnp.concatenate(lefts, axis=1), jnp.concatenate(rights, axis=0))

    def turned(real, imag, sign):
        if sign > 0:
            block = (real[:, :128] + imag[:, 128:], imag[:, :128] - real[:, 128:])
        else:
            block = (real[:, :128] - imag[:, 128:], -imag[:, :128] - real[:, 128:])
        scaled = []
        for part in block:
            scaled += [part[:channels], part[channels:] * scale_ref[...]]
        return jnp.concatenate(scaled, axis=0).T

    for octet in range(2):
        real = total[octet * count : (octet + 1) * count]
        imag = total[(2 + octet) * count : (3 + octet) * count]
        out_ref[octet * 128 : (octet + 1) * 128, :] = turned(real, imag, 1)
        minus = turned(real, imag, -1)
        for place in range(8):
            k = octet * 8 + place
            if k > 0:
                out_ref[(2 * M - k) * M : (2 * M - k + 1) * M, :] = minus[place * M : (place + 1) * M]
    out_ref[M * M : (M + 1) * M, :] = turned(last[:count], last[count:], -1)[:M]


def mid_kernel(
    samples, planes_ref, weight_ref, fx_ref, ix_ref, spread_ref, gather_ref,
    mine_ref, other_ref, out_ref, rows_ref, high_ref, low_ref,
):
    pairs, kept_x, _ = weight_ref.shape
    width_x = planes_ref.shape[0] // pairs
    pack = width_x * pairs // out_ref.shape[0]
    share = kept_x // samples
    me = lax.axis_index("dp")
    lane = lax.broadcasted_iota(jnp.int32, (width_x, 128), 1)
    sign = jnp.where(lane < 64, 1.0, -1.0).astype(F32)
    for step in range(pairs // 2):
        columns = []
        for q in (2 * step, 2 * step + 1):
            plane = planes_ref[pl.ds(q, width_x, stride=pairs), :]
            turned = pltpu.roll(plane, 64, 1) * sign
            columns.append(jnp.concatenate([plane, turned], axis=0))
        high, low = split(jnp.concatenate(columns, axis=1))
        modes = dot(fx_ref[...], jnp.concatenate([high, low, high], axis=0))
        for index, q in enumerate((2 * step, 2 * step + 1)):
            mode = modes[:, index * 128 : (index + 1) * 128]
            rows_ref[q * kept_x : (q + 1) * kept_x, :] = mode
            for ahead in range(samples):
                start = q * kept_x + lax.rem(me + ahead, samples) * share
                part = rows_ref[pl.ds(pl.multiple_of(start, share), share), :]
                if ahead == 0:
                    mine_ref[q] = part
                else:
                    other_ref[(ahead - 1) * pairs + q] = part
    square = weight_ref.shape[2] // 2
    high, low = split(rows_ref[...])
    spread = dot(jnp.concatenate([high, low], axis=1), spread_ref[...])
    for q in range(pairs):
        rows = slice(q * kept_x, (q + 1) * kept_x)
        real, imag = spread[rows, :128], spread[rows, 128:]
        for start in range(0, square, 128):
            w_real = weight_ref[q, :, start : start + 128].astype(F32)
            w_imag = weight_ref[q, :, square + start : square + start + 128].astype(F32)
            first = split(real * w_real + imag * w_imag)
            second = split(imag * w_real - real * w_imag)
            high_ref[rows, start : start + 128] = first[0]
            low_ref[rows, start : start + 128] = first[1]
            high_ref[rows, square + start : square + start + 128] = second[0]
            low_ref[rows, square + start : square + start + 128] = second[1]
    grads = dot(high_ref[...], gather_ref[...]) + dot(low_ref[...], gather_ref[...])
    count = pairs // pack
    if pack == 2:
        size = count * kept_x
        lane = lax.broadcasted_iota(jnp.int32, (size, 256), 1) % 128
        grads = jnp.where(lane < 64, grads[:size], grads[size:])
    for step in range(count // 2):
        columns = []
        for row in (2 * step, 2 * step + 1):
            block = grads[row * kept_x : (row + 1) * kept_x]
            columns.append(jnp.concatenate([block[:, :128], block[:, 128:]], axis=0))
        high, low = split(jnp.concatenate(columns, axis=1))
        planes = dot(ix_ref[...], jnp.concatenate([high, low, high], axis=0))
        for index, row in enumerate((2 * step, 2 * step + 1)):
            out_ref[pl.ds(row, width_x, stride=count), :] = planes[:, index * 128 : (index + 1) * 128]


def weight_kernel(modes_ref, repeat_ref, *refs):
    out_ref = refs[-1]
    pairs, share, _ = modes_ref.shape
    square = out_ref.shape[2] // 2
    chunk = min(pairs, 8)

    @pl.loop(0, pairs // chunk)
    def _(step):
        part = pl.ds(step * chunk, chunk)
        high, low = split(modes_ref[part].reshape(chunk * share, 128))
        side = jnp.concatenate([high, low], axis=1)

        def repeated(start):
            table = repeat_ref[:, start : start + 256]
            return dot(side, jnp.concatenate([table, table], axis=0))

        cots = repeated(2 * square)
        c_real = jnp.concatenate([cots[:, :128]] * 2, axis=1)
        c_imag = jnp.concatenate([cots[:, 128:]] * 2, axis=1)
        for start in range(0, square, 256):
            f_real, f_imag = repeated(start), repeated(square + start)
            real = f_real * c_real + f_imag * c_imag
            imag = f_real * c_imag - f_imag * c_real
            for first, value in ((start, real), (square + start, imag)):
                value = value.reshape(chunk, share, 256)
                for before_ref in refs[:-1]:
                    value = value + before_ref[part, :, first : first + 256]
                out_ref[part, :, first : first + 256] = value


def linear_kernel(cot_ref, weight_ref, linear_ref, mix_ref):
    channels, length_y, length_z = cot_ref.shape
    size = 16 * channels
    left = lax.broadcasted_iota(jnp.int32, (size, channels), 0) // 16 == lax.broadcasted_iota(
        jnp.int32, (size, channels), 1
    )
    right = lax.broadcasted_iota(jnp.int32, (channels, size), 1) // 16 == lax.broadcasted_iota(
        jnp.int32, (channels, size), 0
    )
    tall = dot(left.astype(F32).astype(BF16), weight_ref[...]).astype(BF16)
    wide = dot(tall, right.astype(F32).astype(BF16))
    same = lax.broadcasted_iota(jnp.int32, (size, size), 0) % 16 == lax.broadcasted_iota(
        jnp.int32, (size, size), 1
    ) % 16
    mix_ref[...] = jnp.where(same, wide, 0.0).astype(BF16)
    for step in range(length_y // 32):
        columns = []
        for part in range(2):
            first = step * 32 + part * 16
            columns.append(cot_ref[:, first : first + 16, :].reshape(channels * 16, length_z))
        mixed = dot(mix_ref[...], jnp.concatenate(columns, axis=1))
        for part in range(2):
            first = step * 32 + part * 16
            linear_ref[:, first : first + 16, :] = mixed[:, part * length_z : (part + 1) * length_z].reshape(
                channels, 16, length_z
            )


def inverse_kernel(planes_ref, linear_ref, iz_ref, iy_ref, out_ref, rows_ref):
    channels, _, length_z = linear_ref.shape
    rows = planes_ref.shape[0]
    pack = 2 * M * M // rows
    group = lax.broadcasted_iota(jnp.int32, (16, 256), 1) // M % 8
    keeps = []
    for step in range(4):
        keep = jnp.where(group // 2 == step, 1.0, 0.0).astype(BF16)
        keeps.append(jnp.concatenate([keep] * (channels // 16), axis=0))
    lane = lax.broadcasted_iota(jnp.int32, (M, 128), 1)

    def block(index):
        return planes_ref[index * M : (index + 1) * M, :]

    def halves(turned):
        found = []
        for low_bit in range(pack):
            first = low_bit * 2 * channels
            found.append(
                jnp.concatenate(
                    [turned[first : first + channels], turned[first + channels : first + 2 * channels]], axis=1
                )
            )
        return found

    def along_z(parts, which, steps):
        terms = [split(part) for part in parts]
        left = []
        for step in steps:
            for high, low in terms:
                high, low = high * keeps[step], low * keeps[step]
                left.append(jnp.concatenate([high, low, high], axis=1))
        right = jnp.concatenate([iz_ref[which, 0], iz_ref[which, 0], iz_ref[which, 1]], axis=0)
        return dot(jnp.concatenate(left, axis=0), right)

    def put(value, part, k):
        first = mode_row(part, k) * channels
        rows_ref[first : first + channels, :] = value

    blocks = rows // M
    octets = blocks // 16
    for octet in range(octets):
        sums, differences = [], []
        for place in range(8):
            index = octet * 8 + place
            plus = block(index)
            minus = block(blocks - index) if index > 0 else jnp.zeros_like(plus)
            if pack == 2:
                minus = jnp.where(lane < 64, minus, block(blocks - 1 - index))
            sums.append(plus + minus)
            differences.append(plus - minus)
        for part, stack in enumerate((sums, differences)):
            parts = halves(jnp.concatenate(stack, axis=0).T)
            value = along_z(parts, part, range(4))
            for step in range(4):
                for low_bit in range(pack):
                    first = (step * pack + low_bit) * channels
                    for parity in range(2):
                        k = (octet * 8 + step * 2 + parity) * pack + low_bit
                        put(
                            value[first : first + channels, parity * length_z : (parity + 1) * length_z],
                            part,
                            k,
                        )
    last = block(blocks // 2)
    last = jnp.concatenate([last, jnp.zeros((128 - M, 128), F32)], axis=0).T
    first_half = halves(last)[:1]
    put(along_z(first_half, 0, [0])[:, :length_z], 0, M)
    put(-along_z(first_half, 1, [0])[:, :length_z], 1, M)
    rows_ref[(2 * M + 2) * channels :, :] = jnp.zeros(((ROWS - 2 * M - 2) * channels, length_z), F32)
    for pair in range(channels // 2):
        columns = [rows_ref[pl.ds(2 * pair + side, ROWS, stride=channels), :] for side in range(2)]
        high, low = split(jnp.concatenate(columns, axis=1))
        value = dot(iy_ref[...], jnp.concatenate([high, low, high], axis=0))
        for side in range(2):
            channel = 2 * pair + side
            spectral = value[:, side * length_z : (side + 1) * length_z]
            out_ref[channel] = (spectral + linear_ref[channel]).astype(BF16)


def call(kernel, out_shape, scratch, limit, flops, moved, *args, in_specs=None):
    kwargs = {} if in_specs is None else {"in_specs": in_specs}
    return pl.pallas_call(
        kernel,
        out_shape=out_shape,
        **kwargs,
        scratch_shapes=scratch,
        compiler_params=pltpu.CompilerParams(vmem_limit_bytes=limit * MIB),
        cost_estimate=pl.CostEstimate(flops=flops, bytes_accessed=moved, transcendentals=0),
    )(*args)


def weight_terms(modes, channels):
    parts = modes.reshape(modes.shape[:3] + (2, 2, channels))
    in_real, in_imag = parts[..., 0, 0, :, None], parts[..., 1, 0, :, None]
    cot_real, cot_imag = parts[..., 0, 1, None, :], parts[..., 1, 1, None, :]
    real = jnp.sum(in_real * cot_real + in_imag * cot_imag, axis=0)
    imag = jnp.sum(in_real * cot_imag - in_imag * cot_real, axis=0)
    stacked = jnp.stack([real, imag], axis=2)
    return stacked.reshape(stacked.shape[:2] + (-1,))


def on_device(field, cotangent, spectral_weight, pointwise_weight):
    _, planes, channels, length_y, length_z = field.shape
    pairs, kept_x, _ = spectral_weight.shape
    groups = lax.axis_size("gx")
    samples = lax.axis_size("dp")
    width_x = planes * groups
    share = kept_x // samples
    pack = 2 if pairs == 2 * M else 1
    count = pairs // pack
    all_pairs = 2 * M * M
    cells = width_x * length_y * length_z
    shape = jax.ShapeDtypeStruct
    field = field.reshape(channels, length_y, length_z)
    cotangent = cotangent.reshape(channels, length_y, length_z)

    fy, fz = forward_tables(length_y, length_z)
    iz, iy = inverse_tables(length_y, length_z)
    fx, ix = x_tables(kept_x, width_x)
    scale = np.where(np.arange(M) == 0, 1.0, 2.0) / cells
    scale = np.tile(scale, 8).astype(np.float32)[None]

    spectra = call(
        forward_kernel,
        shape((all_pairs, 128), F32),
        [
            pltpu.VMEM((2,) + field.shape, BF16),
            pltpu.VMEM(scale.shape, F32),
            pltpu.VMEM(fy.shape, BF16),
            pltpu.VMEM(fz.shape, BF16),
            pltpu.VMEM((2 * channels * ROWS, length_z), F32),
            pltpu.SemaphoreType.DMA((7,)),
        ],
        58, 10**9, 5 * 10**6,
        field, cotangent, scale, fy, fz,
        in_specs=[pl.BlockSpec(memory_space=pltpu.HBM)] * 5,
    )
    received = lax.all_to_all(
        spectra.reshape(groups, pairs, 128), "gx", split_axis=0, concat_axis=0, tiled=True
    )
    mine, other, grads = call(
        functools.partial(mid_kernel, samples),
        (
            shape((pairs, share, 128), F32),
            shape((pairs * (samples - 1), share, 128), F32),
            shape((width_x * count, 128), F32),
        ),
        [
            pltpu.VMEM((pairs * kept_x, 128), F32),
            pltpu.VMEM((pairs * kept_x, 2 * channels * channels), BF16),
            pltpu.VMEM((pairs * kept_x, 2 * channels * channels), BF16),
        ],
        16, 10**9, 4 * 10**6,
        received.reshape(width_x * pairs, 128), spectral_weight, fx, ix,
        spread_table(channels), gather_table(channels),
    )
    grads, late_cotangent = lax.optimization_barrier((grads, cotangent))
    linear = call(
        linear_kernel,
        shape((channels, length_y, length_z), F32),
        [pltpu.VMEM((16 * channels, 16 * channels), BF16)],
        16, 2 * 10**9, 3 * 10**6,
        late_cotangent, pointwise_weight,
    )
    returned = lax.all_to_all(
        grads.reshape(groups, count, 128), "gx", split_axis=0, concat_axis=0, tiled=True
    )
    repeat = repeat_table(channels)
    if samples == 2 and share % 8 == 0:
        other = lax.ppermute(other, "dp", [(0, 1), (1, 0)])
        weight_grad = []
        for modes in (mine, other):
            weight_grad = [
                call(
                    weight_kernel,
                    shape((pairs, share, 2 * channels * channels), F32),
                    [],
                    16, 2 * 10**9, 3 * 10**6,
                    modes, repeat, *weight_grad,
                )
            ]
        weight_grad = weight_grad[0]
    else:
        me = lax.axis_index("dp")
        modes = jnp.concatenate([mine[None], other.reshape(samples - 1, pairs, share, 128)])
        modes = jnp.roll(modes, me, 0)
        modes = lax.all_to_all(modes, "dp", split_axis=0, concat_axis=0, tiled=True)
        weight_grad = weight_terms(modes, channels)

    field_grad = call(
        inverse_kernel,
        shape((channels, length_y, length_z), BF16),
        [pltpu.VMEM((ROWS * channels, length_z), F32)],
        16, 10**9, 4 * 10**6,
        returned.reshape(width_x * count, 128), linear, iz, iy,
    )
    return field_grad.reshape(1, planes, channels, length_y, length_z), weight_grad


def solution(mesh):
    placed = (
        P("dp", "gx", None, None, None),
        P("dp", "gx", None, None, None),
        P("gx", None, None),
        P(),
    )
    return jax.shard_map(
        on_device,
        mesh=mesh,
        in_specs=placed,
        out_specs=(P("dp", "gx", None, None, None), P("gx", "dp", None)),
        check_vma=False,
    )
```

```python
import functools
import math

import jax
import jax.numpy as jnp
import ml_dtypes
import numpy as np
from jax import lax
from jax.experimental import pallas as pl
from jax.experimental.pallas import tpu as pltpu
from jax.sharding import PartitionSpec as P

M = 16
F32 = jnp.float32
BF16 = jnp.bfloat16
MIB = 1024 * 1024
ROWS = 3 * M


def kept_freqs(half_count, length):
    index = np.arange(2 * half_count)
    return np.where(index < half_count, index, index + length - 2 * half_count)


def phases(frequency, length):
    product = np.outer(frequency, np.arange(length)) % length
    angle = product * (2.0 * math.pi / length)
    return np.cos(angle), np.sin(angle)


def split_np(table):
    high = table.astype(ml_dtypes.bfloat16)
    low = (table - high.astype(np.float64)).astype(ml_dtypes.bfloat16)
    return high, low


def split(value):
    high = value.astype(BF16)
    low = (value - high.astype(F32)).astype(BF16)
    return high, low


def dot(left, right):
    return jnp.dot(left, right, preferred_element_type=F32)


def forward_tables(length_y, length_z):
    cos_y, sin_y = phases(np.arange(M + 1), length_y)
    rows = np.zeros((ROWS, length_y))
    rows[:M], rows[M : 2 * M] = cos_y[:M], -sin_y[:M]
    rows[2 * M], rows[2 * M + 1] = cos_y[M], -sin_y[M]
    along_y = np.concatenate(split_np(rows), 1)
    cos_z, sin_z = phases(np.arange(M), length_z)
    along_z = np.concatenate([np.tile(cos_z.T, (1, 8)), np.tile(sin_z.T, (1, 8))], 1)
    return along_y, np.stack(split_np(along_z))


def inverse_tables(length_y, length_z):
    cos_z, sin_z = phases(np.arange(M), length_z)
    along_z = np.zeros((2, 2, 8, M, 2, length_z))
    for place in range(8):
        along_z[0, 0, place, :, place % 2] = cos_z
        along_z[0, 1, place, :, place % 2] = -sin_z
        along_z[1, 0, place, :, place % 2] = sin_z
        along_z[1, 1, place, :, place % 2] = cos_z
    along_z = along_z.reshape(2, 2 * 8 * M, 2 * length_z)
    along_z = np.stack([np.stack(split_np(part)) for part in along_z])
    cos_y, sin_y = phases(np.arange(M + 1), length_y)
    columns = np.zeros((length_y, ROWS))
    for k in range(M + 1):
        columns[:, mode_row(0, k)] = cos_y[k]
        columns[:, mode_row(1, k)] = -sin_y[k]
    high, low = split_np(columns)
    return along_z, np.concatenate([high, high, low], 1)


def mode_row(part, k):
    return 2 * M + part if k == M else part * M + k


def x_tables(kept_x, width_x):
    cos_x, sin_x = phases(kept_freqs(kept_x // 2, width_x), width_x)
    high, low = split_np(np.concatenate([cos_x, sin_x], 1))
    forward = np.concatenate([high, high, low], 1)
    high, low = split_np(np.concatenate([cos_x.T, sin_x.T], 1))
    inverse = np.concatenate([high, high, low], 1)
    return forward, inverse


def spread_table(channels):
    copies = 128 // channels
    table = np.zeros((2, 2, 2, channels, 2, copies, channels))
    eye = np.eye(channels)
    for part in range(2):
        table[:, part, 1, :, part] = eye[:, None, :]
    return table.reshape(8 * channels, 256).astype(ml_dtypes.bfloat16)


def gather_table(channels):
    square = channels * channels
    table = np.zeros((2, square // 256, 128, 2, 2, 2, channels))
    for pair in range(square // 256):
        for lane in range(128):
            i = (pair * 256 + (lane % 32 >= 16) * 128 + lane) // channels
            table[0, pair, lane, 0, :, 0, i] = 1.0
            table[1, pair, lane, 0, :, 1, i] = 1.0
            table[1, pair, lane, 1, :, 0, i] = -1.0
            table[0, pair, lane, 1, :, 1, i] = 1.0
    return table.reshape(square, 8 * channels).astype(ml_dtypes.bfloat16)


def repeat_table(channels):
    square = channels * channels
    table = np.zeros((2, 2, channels, 2 * square + 256))
    for i in range(channels):
        for part in range(2):
            start = part * square + i * channels
            table[part, 0, i, start : start + channels] = 1.0
            table[part, 1, i, 2 * square + part * 128 + i : 2 * square + part * 128 + 128 : channels] = 1.0
    return table.reshape(4 * channels, -1).astype(ml_dtypes.bfloat16)


def forward_kernel(
    field_hbm, cot_hbm, scale_hbm, fy_hbm, fz_hbm,
    out_ref, data_ref, scale_ref, fy_ref, fz_ref, rows_ref, sems,
):
    channels, _, length_z = field_hbm.shape
    copies = []

    def start(source, target):
        copy = pltpu.make_async_copy(source, target, sems.at[len(copies)])
        copy.start()
        copies.append(copy)
        return copy

    half = channels // 2
    table_y = start(fy_hbm, fy_ref)
    chunks = []
    for array, ref in enumerate((field_hbm, cot_hbm)):
        for first in (0, half):
            part = pl.ds(first, half)
            chunks.append((array, first, start(ref.at[part], data_ref.at[array, part])))
        if array == 0:
            table_z = start(fz_hbm, fz_ref)
            table_scale = start(scale_hbm, scale_ref)
    table_y.wait()
    for array, first, copy in chunks:
        copy.wait()
        for pair in range(first // 2, (first + half) // 2):
            data = jnp.concatenate([data_ref[array, 2 * pair], data_ref[array, 2 * pair + 1]], axis=1)
            value = dot(fy_ref[...], jnp.concatenate([data, data], axis=0))
            base = (array * channels + 2 * pair) * ROWS
            rows_ref[base : base + ROWS, :] = value[:, :length_z]
            rows_ref[base + ROWS : base + 2 * ROWS, :] = value[:, length_z:]
    table_z.wait()
    table_scale.wait()
    count = 2 * channels
    group = lax.broadcasted_iota(jnp.int32, (16, 256), 1) // M % 8
    lefts, rights = [], []
    for place in range(8):
        keep = jnp.where(group == place, 1.0, 0.0).astype(BF16)
        keep = jnp.concatenate([keep] * (length_z // 16), axis=0)
        table_high, table_low = fz_ref[0] * keep, fz_ref[1] * keep
        sources = [part * M + octet * 8 + place for part in range(2) for octet in range(2)]
        if place == 0:
            sources += [2 * M, 2 * M + 1]
        rows = [rows_ref[pl.ds(source, count, stride=ROWS), :] for source in sources]
        high, low = split(jnp.concatenate(rows, axis=0))
        left = jnp.concatenate([high, low, high], axis=1)
        right = jnp.concatenate([table_high, table_high, table_low], axis=0)
        if place == 0:
            last = dot(left[4 * count :], right)
            left = left[: 4 * count]
        lefts.append(left)
        rights.append(right)
    total = dot(jnp.concatenate(lefts, axis=1), jnp.concatenate(rights, axis=0))

    def turned(real, imag, sign):
        if sign > 0:
            block = (real[:, :128] + imag[:, 128:], imag[:, :128] - real[:, 128:])
        else:
            block = (real[:, :128] - imag[:, 128:], -imag[:, :128] - real[:, 128:])
        scaled = []
        for part in block:
            scaled += [part[:channels], part[channels:] * scale_ref[...]]
        return jnp.concatenate(scaled, axis=0).T

    for octet in range(2):
        real = total[octet * count : (octet + 1) * count]
        imag = total[(2 + octet) * count : (3 + octet) * count]
        out_ref[octet * 128 : (octet + 1) * 128, :] = turned(real, imag, 1)
        minus = turned(real, imag, -1)
        for place in range(8):
            k = octet * 8 + place
            if k > 0:
                out_ref[(2 * M - k) * M : (2 * M - k + 1) * M, :] = minus[place * M : (place + 1) * M]
    out_ref[M * M : (M + 1) * M, :] = turned(last[:count], last[count:], -1)[:M]


def mid_kernel(
    samples, planes_ref, weight_ref, fx_ref, ix_ref, spread_ref, gather_ref,
    mine_ref, other_ref, out_ref, rows_ref, split_ref,
):
    pairs, kept_x, _ = weight_ref.shape
    width_x = planes_ref.shape[0] // pairs
    pack = width_x * pairs // out_ref.shape[0]
    share = kept_x // samples
    me = lax.axis_index("dp")
    lane = lax.broadcasted_iota(jnp.int32, (width_x, 128), 1)
    sign = jnp.where(lane < 64, 1.0, -1.0).astype(F32)
    for step in range(pairs // 2):
        columns = []
        for q in (2 * step, 2 * step + 1):
            plane = planes_ref[pl.ds(q, width_x, stride=pairs), :]
            turned = pltpu.roll(plane, 64, 1) * sign
            columns.append(jnp.concatenate([plane, turned], axis=0))
        high, low = split(jnp.concatenate(columns, axis=1))
        modes = dot(fx_ref[...], jnp.concatenate([high, low, high], axis=0))
        for index, q in enumerate((2 * step, 2 * step + 1)):
            mode = modes[:, index * 128 : (index + 1) * 128]
            rows_ref[q * kept_x : (q + 1) * kept_x, :] = mode
            for ahead in range(samples):
                start = q * kept_x + lax.rem(me + ahead, samples) * share
                part = rows_ref[pl.ds(pl.multiple_of(start, share), share), :]
                if ahead == 0:
                    mine_ref[q] = part
                else:
                    other_ref[(ahead - 1) * pairs + q] = part

    square = weight_ref.shape[2] // 2
    lane = lax.broadcasted_iota(jnp.int32, (kept_x, 128), 1) % 32
    first_half = lane < 16

    def halved(one, two):
        kept = jnp.where(first_half, one, two)
        moved = jnp.where(first_half, two, one)
        return kept + jnp.where(first_half, pltpu.roll(moved, 112, 1), pltpu.roll(moved, 16, 1))

    def products(rows, q, start):
        real, imag = rows[:, :128], rows[:, 128:]
        w_real = weight_ref[q, :, start : start + 128].astype(F32)
        w_imag = weight_ref[q, :, square + start : square + start + 128].astype(F32)
        return real * w_real + imag * w_imag, imag * w_real - real * w_imag

    grads = []
    chunk = 8
    for first in range(0, pairs, chunk):
        high, low = split(rows_ref[first * kept_x : (first + chunk) * kept_x, :])
        spread = dot(jnp.concatenate([high, low], axis=1), spread_ref[...])
        size = chunk * kept_x
        base = 2 * first * kept_x
        for place in range(chunk):
            rows = spread[place * kept_x : (place + 1) * kept_x]
            at = base + place * kept_x
            for start in range(0, square, 256):
                ones = products(rows, first + place, start)
                twos = products(rows, first + place, start + 128)
                for part in range(2):
                    column = (part * square + start) // 2
                    high, low = split(halved(ones[part], twos[part]))
                    split_ref[at : at + kept_x, column : column + 128] = high
                    split_ref[at + size : at + size + kept_x, column : column + 128] = low
        both = dot(split_ref[base : base + 2 * size, :], gather_ref[...])
        grads.append(both[:size] + both[size:])
    grads = jnp.concatenate(grads, axis=0)
    count = pairs // pack
    if pack == 2:
        size = count * kept_x
        lane = lax.broadcasted_iota(jnp.int32, (size, 256), 1) % 128
        grads = jnp.where(lane < 64, grads[:size], grads[size:])
    for step in range(count // 2):
        columns = []
        for row in (2 * step, 2 * step + 1):
            block = grads[row * kept_x : (row + 1) * kept_x]
            columns.append(jnp.concatenate([block[:, :128], block[:, 128:]], axis=0))
        high, low = split(jnp.concatenate(columns, axis=1))
        planes = dot(ix_ref[...], jnp.concatenate([high, low, high], axis=0))
        for index, row in enumerate((2 * step, 2 * step + 1)):
            out_ref[pl.ds(row, width_x, stride=count), :] = planes[:, index * 128 : (index + 1) * 128]


def weight_terms_in(modes_ref, repeat_ref, part, emit):
    square = (repeat_ref.shape[1] - 256) // 2
    rows = modes_ref[part]
    shape = rows.shape[:2] + (256,)
    high, low = split(rows.reshape(shape[0] * shape[1], 128))
    side = jnp.concatenate([high, low], axis=1)

    def repeated(start):
        table = repeat_ref[:, start : start + 256]
        return dot(side, jnp.concatenate([table, table], axis=0))

    cots = repeated(2 * square)
    c_real = jnp.concatenate([cots[:, :128]] * 2, axis=1)
    c_imag = jnp.concatenate([cots[:, 128:]] * 2, axis=1)
    for start in range(0, square, 256):
        f_real, f_imag = repeated(start), repeated(square + start)
        emit(start, (f_real * c_real + f_imag * c_imag).reshape(shape))
        emit(square + start, (f_real * c_imag - f_imag * c_real).reshape(shape))


def weight_kernel(modes_ref, repeat_ref, before_ref, out_hbm, out_ref, sems):
    pairs = modes_ref.shape[0]
    copies = []
    for first in range(0, pairs, pairs // 4):
        part = pl.ds(first, pairs // 4)

        def emit(start, value):
            out_ref[part, :, start : start + 256] = before_ref[part, :, start : start + 256] + value

        weight_terms_in(modes_ref, repeat_ref, part, emit)
        copies.append(pltpu.make_async_copy(out_ref.at[part], out_hbm.at[part], sems.at[len(copies)]))
        copies[-1].start()
    for copy in copies:
        copy.wait()


def local_kernel(kept, *refs):
    cot_hbm, weight_ref = refs[:2]
    linear_ref, cot_ref, mix_ref, sem = refs[kept + 2], *refs[-3:]
    copy = pltpu.make_async_copy(cot_hbm, cot_ref, sem)
    copy.start()
    if kept:
        modes_ref, repeat_ref, out_ref = refs[2], refs[3], refs[5]
        pairs = modes_ref.shape[0]
        for first in range(0, pairs, pairs // 4):
            part = pl.ds(first, pairs // 4)

            def emit(start, value):
                out_ref[part, :, start : start + 256] = value

            weight_terms_in(modes_ref, repeat_ref, part, emit)
    channels, length_y, length_z = cot_ref.shape
    size = 16 * channels
    left = lax.broadcasted_iota(jnp.int32, (size, channels), 0) // 16 == lax.broadcasted_iota(
        jnp.int32, (size, channels), 1
    )
    right = lax.broadcasted_iota(jnp.int32, (channels, size), 1) // 16 == lax.broadcasted_iota(
        jnp.int32, (channels, size), 0
    )
    tall = dot(left.astype(F32).astype(BF16), weight_ref[...]).astype(BF16)
    wide = dot(tall, right.astype(F32).astype(BF16))
    same = lax.broadcasted_iota(jnp.int32, (size, size), 0) % 16 == lax.broadcasted_iota(
        jnp.int32, (size, size), 1
    ) % 16
    mix_ref[...] = jnp.where(same, wide, 0.0).astype(BF16)
    copy.wait()
    for step in range(length_y // 32):
        columns = []
        for part in range(2):
            first = step * 32 + part * 16
            columns.append(cot_ref[:, first : first + 16, :].reshape(channels * 16, length_z))
        mixed = dot(mix_ref[...], jnp.concatenate(columns, axis=1))
        for part in range(2):
            first = step * 32 + part * 16
            linear_ref[:, first : first + 16, :] = mixed[:, part * length_z : (part + 1) * length_z].reshape(
                channels, 16, length_z
            )


def inverse_kernel(planes_ref, linear_ref, iz_ref, iy_ref, out_hbm, rows_ref, out_ref, sems):
    channels, _, length_z = linear_ref.shape
    rows = planes_ref.shape[0]
    pack = 2 * M * M // rows
    group = lax.broadcasted_iota(jnp.int32, (16, 256), 1) // M % 8
    keeps = []
    for step in range(4):
        keep = jnp.where(group // 2 == step, 1.0, 0.0).astype(BF16)
        keeps.append(jnp.concatenate([keep] * (channels // 16), axis=0))
    lane = lax.broadcasted_iota(jnp.int32, (M, 128), 1)

    def block(index):
        return planes_ref[index * M : (index + 1) * M, :]

    def halves(turned):
        found = []
        for low_bit in range(pack):
            first = low_bit * 2 * channels
            found.append(
                jnp.concatenate(
                    [turned[first : first + channels], turned[first + channels : first + 2 * channels]], axis=1
                )
            )
        return found

    def along_z(parts, which, steps):
        terms = [split(part) for part in parts]
        left = []
        for step in steps:
            for high, low in terms:
                high, low = high * keeps[step], low * keeps[step]
                left.append(jnp.concatenate([high, low, high], axis=1))
        right = jnp.concatenate([iz_ref[which, 0], iz_ref[which, 0], iz_ref[which, 1]], axis=0)
        return dot(jnp.concatenate(left, axis=0), right)

    def put(value, part, k):
        first = mode_row(part, k) * channels
        rows_ref[first : first + channels, :] = value

    blocks = rows // M
    octets = blocks // 16
    for octet in range(octets):
        sums, differences = [], []
        for place in range(8):
            index = octet * 8 + place
            plus = block(index)
            minus = block(blocks - index) if index > 0 else jnp.zeros_like(plus)
            if pack == 2:
                minus = jnp.where(lane < 64, minus, block(blocks - 1 - index))
            sums.append(plus + minus)
            differences.append(plus - minus)
        for part, stack in enumerate((sums, differences)):
            parts = halves(jnp.concatenate(stack, axis=0).T)
            value = along_z(parts, part, range(4))
            for step in range(4):
                for low_bit in range(pack):
                    first = (step * pack + low_bit) * channels
                    for parity in range(2):
                        k = (octet * 8 + step * 2 + parity) * pack + low_bit
                        put(
                            value[first : first + channels, parity * length_z : (parity + 1) * length_z],
                            part,
                            k,
                        )
    last = block(blocks // 2)
    last = jnp.concatenate([last, jnp.zeros((128 - M, 128), F32)], axis=0).T
    first_half = halves(last)[:1]
    put(along_z(first_half, 0, [0])[:, :length_z], 0, M)
    put(-along_z(first_half, 1, [0])[:, :length_z], 1, M)
    rows_ref[(2 * M + 2) * channels :, :] = jnp.zeros(((ROWS - 2 * M - 2) * channels, length_z), F32)
    copies = []
    for pair in range(channels // 2):
        columns = [rows_ref[pl.ds(2 * pair + side, ROWS, stride=channels), :] for side in range(2)]
        high, low = split(jnp.concatenate(columns, axis=1))
        value = dot(iy_ref[...], jnp.concatenate([high, low, high], axis=0))
        for side in range(2):
            channel = 2 * pair + side
            spectral = value[:, side * length_z : (side + 1) * length_z]
            out_ref[channel] = (spectral + linear_ref[channel]).astype(BF16)
        if pair % 4 == 3:
            part = pl.ds(2 * pair - 6, 8)
            copies.append(pltpu.make_async_copy(out_ref.at[part], out_hbm.at[part], sems.at[len(copies)]))
            copies[-1].start()
    for copy in copies:
        copy.wait()


def in_hbm(value):
    return pltpu.with_memory_space_constraint(value, pltpu.HBM)


def call(kernel, out_shape, scratch, limit, flops, moved, *args, **kwargs):
    return pl.pallas_call(
        kernel,
        out_shape=out_shape,
        **kwargs,
        scratch_shapes=scratch,
        compiler_params=pltpu.CompilerParams(vmem_limit_bytes=limit * MIB),
        cost_estimate=pl.CostEstimate(flops=flops, bytes_accessed=moved, transcendentals=0),
    )(*args)


def weight_terms(modes, channels):
    parts = modes.reshape(modes.shape[:3] + (2, 2, channels))
    in_real, in_imag = parts[..., 0, 0, :, None], parts[..., 1, 0, :, None]
    cot_real, cot_imag = parts[..., 0, 1, None, :], parts[..., 1, 1, None, :]
    real = jnp.sum(in_real * cot_real + in_imag * cot_imag, axis=0)
    imag = jnp.sum(in_real * cot_imag - in_imag * cot_real, axis=0)
    stacked = jnp.stack([real, imag], axis=2)
    return stacked.reshape(stacked.shape[:2] + (-1,))


def on_device(field, cotangent, spectral_weight, pointwise_weight):
    _, planes, channels, length_y, length_z = field.shape
    pairs, kept_x, _ = spectral_weight.shape
    groups = lax.axis_size("gx")
    samples = lax.axis_size("dp")
    width_x = planes * groups
    share = kept_x // samples
    pack = 2 if pairs == 2 * M else 1
    count = pairs // pack
    all_pairs = 2 * M * M
    cells = width_x * length_y * length_z
    shape = jax.ShapeDtypeStruct
    field = field.reshape(channels, length_y, length_z)
    cotangent = cotangent.reshape(channels, length_y, length_z)

    fy, fz = forward_tables(length_y, length_z)
    iz, iy = inverse_tables(length_y, length_z)
    fx, ix = x_tables(kept_x, width_x)
    scale = np.where(np.arange(M) == 0, 1.0, 2.0) / cells
    scale = np.tile(scale, 8).astype(np.float32)[None]

    hbm = pl.BlockSpec(memory_space=pltpu.HBM)
    spectra = call(
        forward_kernel,
        pltpu.VMEM((all_pairs, 128), F32),
        [
            pltpu.VMEM((2,) + field.shape, BF16),
            pltpu.VMEM(scale.shape, F32),
            pltpu.VMEM(fy.shape, BF16),
            pltpu.VMEM(fz.shape, BF16),
            pltpu.VMEM((2 * channels * ROWS, length_z), F32),
            pltpu.SemaphoreType.DMA((7,)),
        ],
        16, 10**9, 5 * 10**6,
        *[in_hbm(one) for one in (field, cotangent, scale, fy, fz)],
        in_specs=[hbm] * 5,
    )
    spectra, spectral_weight, spread, gather = lax.optimization_barrier(
        (spectra, spectral_weight, spread_table(channels), gather_table(channels))
    )
    received = lax.all_to_all(
        spectra.reshape(groups, pairs, 128), "gx", split_axis=0, concat_axis=0, tiled=True
    )
    mine, other, grads = call(
        functools.partial(mid_kernel, samples),
        (
            pltpu.VMEM((pairs, share, 128), F32),
            pltpu.VMEM((pairs * (samples - 1), share, 128), F32),
            pltpu.VMEM((width_x * count, 128), F32),
        ),
        [
            pltpu.VMEM((pairs * kept_x, 128), F32),
            pltpu.VMEM((2 * pairs * kept_x, channels * channels), BF16),
        ],
        16, 10**9, 4 * 10**6,
        received.reshape(width_x * pairs, 128), spectral_weight, fx, ix, spread, gather,
    )
    returned = lax.all_to_all(
        grads.reshape(groups, count, 128), "gx", split_axis=0, concat_axis=0, tiled=True
    )
    split_samples = samples == 2 and share % 8 == 0
    kept = [mine, repeat_table(channels)] if split_samples else []
    tall = (pairs, share, 2 * channels * channels)
    _, late = lax.optimization_barrier((grads, cotangent))
    linear, *weight_grad = call(
        functools.partial(local_kernel, len(kept)),
        [shape((channels, length_y, length_z), F32)] + [shape(tall, F32)] * (len(kept) // 2),
        [
            pltpu.VMEM((channels, length_y, length_z), BF16),
            pltpu.VMEM((16 * channels, 16 * channels), BF16),
            pltpu.SemaphoreType.DMA(()),
        ],
        16, 4 * 10**9, 5 * 10**6,
        in_hbm(late), pointwise_weight, *kept,
        in_specs=[hbm] + [pl.BlockSpec()] * (1 + len(kept)),
    )
    if split_samples:
        other = lax.ppermute(other, "dp", [(0, 1), (1, 0)])
        weight_grad = call(
            weight_kernel,
            shape(tall, F32),
            [pltpu.VMEM(tall, F32), pltpu.SemaphoreType.DMA((4,))],
            16, 2 * 10**9, 5 * 10**6,
            other, kept[1], *weight_grad,
            out_specs=hbm,
        )
    else:
        me = lax.axis_index("dp")
        modes = jnp.concatenate([mine[None], other.reshape(samples - 1, pairs, share, 128)])
        modes = jnp.roll(modes, me, 0)
        modes = lax.all_to_all(modes, "dp", split_axis=0, concat_axis=0, tiled=True)
        weight_grad = weight_terms(modes, channels)
    field_grad = call(
        inverse_kernel,
        shape((channels, length_y, length_z), BF16),
        [
            pltpu.VMEM((ROWS * channels, length_z), F32),
            pltpu.VMEM((channels, length_y, length_z), BF16),
            pltpu.SemaphoreType.DMA((channels // 8,)),
        ],
        16, 10**9, 4 * 10**6,
        returned.reshape(width_x * count, 128), linear, iz, iy,
        out_specs=hbm,
    )
    return field_grad.reshape(1, planes, channels, length_y, length_z), weight_grad


def solution(mesh):
    placed = (
        P("dp", "gx", None, None, None),
        P("dp", "gx", None, None, None),
        P("gx", None, None),
        P(),
    )
    return jax.shard_map(
        on_device,
        mesh=mesh,
        in_specs=placed,
        out_specs=(P("dp", "gx", None, None, None), P("gx", "dp", None)),
        check_vma=False,
    )
```

```python
import functools
import math

import jax
import jax.numpy as jnp
import ml_dtypes
import numpy as np
from jax import lax
from jax.experimental import pallas as pl
from jax.experimental.pallas import tpu as pltpu
from jax.sharding import PartitionSpec as P

M = 16
F32 = jnp.float32
BF16 = jnp.bfloat16
MIB = 1024 * 1024
ROWS = 3 * M
PITCH = ROWS - 8


def kept_freqs(half_count, length):
    index = np.arange(2 * half_count)
    return np.where(index < half_count, index, index + length - 2 * half_count)


def phases(frequency, length):
    product = np.outer(frequency, np.arange(length)) % length
    angle = product * (2.0 * math.pi / length)
    return np.cos(angle), np.sin(angle)


def split_np(table):
    high = table.astype(ml_dtypes.bfloat16)
    low = (table - high.astype(np.float64)).astype(ml_dtypes.bfloat16)
    return high, low


def split(value):
    high = value.astype(BF16)
    low = (value - high.astype(F32)).astype(BF16)
    return high, low


def dot(left, right):
    return jnp.dot(left, right, preferred_element_type=F32)


def forward_tables(length_y, length_z):
    cos_y, sin_y = phases(np.arange(M + 1), length_y)
    rows = np.zeros((ROWS, length_y))
    rows[:M], rows[M : 2 * M] = cos_y[:M], -sin_y[:M]
    rows[2 * M], rows[2 * M + 1] = cos_y[M], -sin_y[M]
    along_y = np.concatenate(split_np(rows), 0)
    cos_z, sin_z = phases(np.arange(M), length_z)
    along_z = np.concatenate([np.tile(cos_z.T, (1, 8)), np.tile(sin_z.T, (1, 8))], 1)
    return along_y, np.stack(split_np(along_z))


def inverse_tables(length_y, length_z):
    cos_z, sin_z = phases(np.arange(M), length_z)
    along_z = np.zeros((2, 2, 8, M, 2, length_z))
    for place in range(8):
        along_z[0, 0, place, :, place % 2] = cos_z
        along_z[0, 1, place, :, place % 2] = -sin_z
        along_z[1, 0, place, :, place % 2] = sin_z
        along_z[1, 1, place, :, place % 2] = cos_z
    along_z = along_z.reshape(2, 2 * 8 * M, 2 * length_z)
    along_z = np.stack([np.stack(split_np(part)) for part in along_z])
    cos_y, sin_y = phases(np.arange(M + 1), length_y)
    columns = np.zeros((length_y, ROWS))
    for k in range(M + 1):
        columns[:, mode_row(0, k)] = cos_y[k]
        columns[:, mode_row(1, k)] = -sin_y[k]
    high, low = split_np(columns)
    return along_z, np.concatenate([high, high, low], 1)


def mode_row(part, k):
    return 2 * M + part if k == M else part * M + k


def x_tables(kept_x, width_x):
    cos_x, sin_x = phases(kept_freqs(kept_x // 2, width_x), width_x)
    high, low = split_np(np.concatenate([cos_x, sin_x], 1))
    forward = np.concatenate([high, high, low], 1)
    high, low = split_np(np.concatenate([cos_x.T, sin_x.T], 1))
    inverse = np.concatenate([high, high, low], 1)
    return forward, inverse


def spread_table(channels):
    copies = 128 // channels
    table = np.zeros((2, 2, 2, channels, 2, copies, channels))
    eye = np.eye(channels)
    for part in range(2):
        table[:, part, 1, :, part] = eye[:, None, :]
    return table.reshape(8 * channels, 256).astype(ml_dtypes.bfloat16)


LEVELS = 1


def gather_table(channels):
    width = channels * channels >> LEVELS
    place = np.arange(width)
    block, lane = place // 128, place % 128
    step = block << LEVELS
    for level in range(LEVELS):
        step = step + ((lane & 16 >> level) > 0) * (1 << level)
    i = step * (128 // channels) + lane // channels
    table = np.zeros((2, width, 2, 2, 2, channels))
    for part in range(2):
        table[part, place, 0, :, part, i] = 1.0
        table[part, place, 1, :, 1 - part, i] = 1.0 - 2.0 * part
    return table.reshape(2 * width, 8 * channels).astype(ml_dtypes.bfloat16)


def repeat_table(channels):
    square = channels * channels
    table = np.zeros((2, 2, channels, 2 * square + 256))
    for i in range(channels):
        for part in range(2):
            start = part * square + i * channels
            table[part, 0, i, start : start + channels] = 1.0
            table[part, 1, i, 2 * square + part * 128 + i : 2 * square + part * 128 + 128 : channels] = 1.0
    return table.reshape(4 * channels, -1).astype(ml_dtypes.bfloat16)


def forward_kernel(
    field_hbm, cot_hbm, scale_hbm, fy_hbm, fz_hbm,
    out_ref, data_ref, scale_ref, fy_ref, fz_ref, spread_ref, rows_ref, sems,
):
    channels, _, length_z = field_hbm.shape
    copies = []

    def start(source, target):
        copy = pltpu.make_async_copy(source, target, sems.at[len(copies)])
        copy.start()
        copies.append(copy)
        return copy

    half = channels // 2
    table_z = start(fz_hbm, fz_ref)
    table_y = start(fy_hbm, fy_ref)
    chunks = []
    for array, ref in enumerate((field_hbm, cot_hbm)):
        for first in (0, half):
            part = pl.ds(first, half)
            chunks.append((array, first, start(ref.at[part], data_ref.at[array, part])))
    table_scale = start(scale_hbm, scale_ref)
    table_z.wait()
    group = lax.broadcasted_iota(jnp.int32, (16, 256), 1) // M % 8
    for place in range(8):
        keep = jnp.where(group == place, 1.0, 0.0).astype(BF16)
        keep = jnp.concatenate([keep] * (length_z // 16), axis=0)
        for term in range(2):
            spread_ref[place, term * length_z : (term + 1) * length_z, :] = fz_ref[term] * keep
    table_y.wait()
    for array, first, copy in chunks:
        copy.wait()
        for pair in range(first // 2, (first + half) // 2):
            data = jnp.concatenate([data_ref[array, 2 * pair], data_ref[array, 2 * pair + 1]], axis=1)
            both = dot(fy_ref[...], data)
            value = both[:PITCH] + both[ROWS : ROWS + PITCH]
            base = (array * channels + 2 * pair) * PITCH
            rows_ref[base : base + PITCH, :] = value[:, :length_z]
            rows_ref[base + PITCH : base + 2 * PITCH, :] = value[:, length_z:]
    table_scale.wait()
    count = 2 * channels
    lefts, rights = [], []
    for place in range(8):
        table_high, table_low = spread_ref[place, :length_z], spread_ref[place, length_z:]
        sources = [part * M + octet * 8 + place for part in range(2) for octet in range(2)]
        if place == 0:
            sources += [2 * M, 2 * M + 1]
        rows = [rows_ref[pl.ds(source, count, stride=PITCH), :] for source in sources]
        high, low = split(jnp.concatenate(rows, axis=0))
        left = jnp.concatenate([high, low, high], axis=1)
        right = jnp.concatenate([table_high, table_high, table_low], axis=0)
        if place == 0:
            last = dot(left[4 * count :], right)
            left = left[: 4 * count]
        lefts.append(left)
        rights.append(right)
    total = dot(jnp.concatenate(lefts, axis=1), jnp.concatenate(rights, axis=0))

    def turned(real, imag, sign):
        if sign > 0:
            block = (real[:, :128] + imag[:, 128:], imag[:, :128] - real[:, 128:])
        else:
            block = (real[:, :128] - imag[:, 128:], -imag[:, :128] - real[:, 128:])
        scaled = []
        for part in block:
            scaled += [part[:channels], part[channels:] * scale_ref[...]]
        return jnp.concatenate(scaled, axis=0).T

    for octet in range(2):
        real = total[octet * count : (octet + 1) * count]
        imag = total[(2 + octet) * count : (3 + octet) * count]
        out_ref[octet * 128 : (octet + 1) * 128, :] = turned(real, imag, 1)
        minus = turned(real, imag, -1)
        for place in range(8):
            k = octet * 8 + place
            if k > 0:
                out_ref[(2 * M - k) * M : (2 * M - k + 1) * M, :] = minus[place * M : (place + 1) * M]
    out_ref[M * M : (M + 1) * M, :] = turned(last[:count], last[count:], -1)[:M]


def mid_kernel(
    samples, planes_ref, weight_ref, fx_ref, ix_ref, spread_ref, gather_ref,
    mine_ref, other_ref, out_ref, rows_ref, split_ref,
):
    pairs, kept_x, _ = weight_ref.shape
    width_x = planes_ref.shape[0] // pairs
    pack = width_x * pairs // out_ref.shape[0]
    share = kept_x // samples
    me = lax.axis_index("dp")
    lane = lax.broadcasted_iota(jnp.int32, (width_x, 128), 1)
    sign = jnp.where(lane < 64, 1.0, -1.0).astype(F32)
    for step in range(pairs // 2):
        columns = []
        for q in (2 * step, 2 * step + 1):
            plane = planes_ref[pl.ds(q, width_x, stride=pairs), :]
            turned = pltpu.roll(plane, 64, 1) * sign
            columns.append(jnp.concatenate([plane, turned], axis=0))
        high, low = split(jnp.concatenate(columns, axis=1))
        modes = dot(fx_ref[...], jnp.concatenate([high, low, high], axis=0))
        for index, q in enumerate((2 * step, 2 * step + 1)):
            mode = modes[:, index * 128 : (index + 1) * 128]
            rows_ref[q * kept_x : (q + 1) * kept_x, :] = mode
            for ahead in range(samples):
                start = q * kept_x + lax.rem(me + ahead, samples) * share
                part = rows_ref[pl.ds(pl.multiple_of(start, share), share), :]
                if ahead == 0:
                    mine_ref[q] = part
                else:
                    other_ref[(ahead - 1) * pairs + q] = part

    square = weight_ref.shape[2] // 2
    width = square >> LEVELS
    lane = lax.broadcasted_iota(jnp.int32, (kept_x, 128), 1)

    def merge(one, two, shift):
        first = lane & shift == 0
        moved = jnp.where(first, two, one)
        moved = jnp.take_along_axis(moved, lane ^ shift, axis=1, mode="promise_in_bounds")
        return jnp.where(first, one, two) + moved

    def products(rows, q, start):
        real, imag = rows[:, :128], rows[:, 128:]
        w_real = weight_ref[q, :, start : start + 128].astype(F32)
        w_imag = weight_ref[q, :, square + start : square + start + 128].astype(F32)
        return real * w_real + imag * w_imag, imag * w_real - real * w_imag

    grads = []
    chunk = 8
    for first in range(0, pairs, chunk):
        high, low = split(rows_ref[first * kept_x : (first + chunk) * kept_x, :])
        spread = dot(jnp.concatenate([high, low], axis=1), spread_ref[...])
        size = chunk * kept_x
        base = 2 * first * kept_x
        for place in range(chunk):
            rows = spread[place * kept_x : (place + 1) * kept_x]
            at = base + place * kept_x
            for column in range(0, width, 128):
                items = [
                    products(rows, first + place, start)
                    for start in range(column << LEVELS, column + 128 << LEVELS, 128)
                ]
                for part in range(2):
                    values = [item[part] for item in items]
                    for level in range(LEVELS):
                        values = [merge(one, two, 16 >> level) for one, two in zip(values[::2], values[1::2])]
                    high, low = split(values[0])
                    at_column = part * width + column
                    split_ref[at : at + kept_x, at_column : at_column + 128] = high
                    split_ref[at + size : at + size + kept_x, at_column : at_column + 128] = low
        both = dot(split_ref[base : base + 2 * size, :], gather_ref[...])
        grads.append(both[:size] + both[size:])
    grads = jnp.concatenate(grads, axis=0)
    count = pairs // pack
    if pack == 2:
        size = count * kept_x
        lane = lax.broadcasted_iota(jnp.int32, (size, 256), 1) % 128
        grads = jnp.where(lane < 64, grads[:size], grads[size:])
    for step in range(count // 2):
        columns = []
        for row in (2 * step, 2 * step + 1):
            block = grads[row * kept_x : (row + 1) * kept_x]
            columns.append(jnp.concatenate([block[:, :128], block[:, 128:]], axis=0))
        high, low = split(jnp.concatenate(columns, axis=1))
        planes = dot(ix_ref[...], jnp.concatenate([high, low, high], axis=0))
        for index, row in enumerate((2 * step, 2 * step + 1)):
            out_ref[pl.ds(row, width_x, stride=count), :] = planes[:, index * 128 : (index + 1) * 128]


def weight_terms_in(modes_ref, repeat_ref, part, emit):
    square = (repeat_ref.shape[1] - 256) // 2
    rows = modes_ref[part]
    shape = rows.shape[:2] + (256,)
    high, low = split(rows.reshape(shape[0] * shape[1], 128))
    side = jnp.concatenate([high, low], axis=1)

    def repeated(start):
        table = repeat_ref[:, start : start + 256]
        return dot(side, jnp.concatenate([table, table], axis=0))

    cots = repeated(2 * square)
    c_real = jnp.concatenate([cots[:, :128]] * 2, axis=1)
    c_imag = jnp.concatenate([cots[:, 128:]] * 2, axis=1)
    for start in range(0, square, 256):
        f_real, f_imag = repeated(start), repeated(square + start)
        emit(start, (f_real * c_real + f_imag * c_imag).reshape(shape))
        emit(square + start, (f_real * c_imag - f_imag * c_real).reshape(shape))


def weight_kernel(modes_ref, repeat_ref, before_ref, out_hbm, out_ref, sems):
    pairs = modes_ref.shape[0]
    copies = []
    for first in range(0, pairs, pairs // 4):
        part = pl.ds(first, pairs // 4)

        def emit(start, value):
            out_ref[part, :, start : start + 256] = before_ref[part, :, start : start + 256] + value

        weight_terms_in(modes_ref, repeat_ref, part, emit)
        copies.append(pltpu.make_async_copy(out_ref.at[part], out_hbm.at[part], sems.at[len(copies)]))
        copies[-1].start()
    for copy in copies:
        copy.wait()


def local_kernel(kept, *refs):
    cot_hbm, weight_ref = refs[:2]
    linear_ref, cot_ref, mix_ref, sem = refs[kept + 2], *refs[-3:]
    copy = pltpu.make_async_copy(cot_hbm, cot_ref, sem)
    copy.start()
    if kept:
        modes_ref, repeat_ref, out_ref = refs[2], refs[3], refs[5]
        pairs = modes_ref.shape[0]
        for first in range(0, pairs, pairs // 4):
            part = pl.ds(first, pairs // 4)

            def emit(start, value):
                out_ref[part, :, start : start + 256] = value

            weight_terms_in(modes_ref, repeat_ref, part, emit)
    channels, length_y, length_z = cot_ref.shape
    size = 16 * channels
    left = lax.broadcasted_iota(jnp.int32, (size, channels), 0) // 16 == lax.broadcasted_iota(
        jnp.int32, (size, channels), 1
    )
    right = lax.broadcasted_iota(jnp.int32, (channels, size), 1) // 16 == lax.broadcasted_iota(
        jnp.int32, (channels, size), 0
    )
    tall = dot(left.astype(F32).astype(BF16), weight_ref[...]).astype(BF16)
    wide = dot(tall, right.astype(F32).astype(BF16))
    same = lax.broadcasted_iota(jnp.int32, (size, size), 0) % 16 == lax.broadcasted_iota(
        jnp.int32, (size, size), 1
    ) % 16
    mix_ref[...] = jnp.where(same, wide, 0.0).astype(BF16)
    copy.wait()
    for step in range(length_y // 32):
        columns = []
        for part in range(2):
            first = step * 32 + part * 16
            columns.append(cot_ref[:, first : first + 16, :].reshape(channels * 16, length_z))
        mixed = dot(mix_ref[...], jnp.concatenate(columns, axis=1))
        for part in range(2):
            first = step * 32 + part * 16
            linear_ref[:, first : first + 16, :] = mixed[:, part * length_z : (part + 1) * length_z].reshape(
                channels, 16, length_z
            )


def inverse_kernel(planes_ref, linear_ref, iz_ref, iy_ref, out_hbm, rows_ref, out_ref, sems):
    channels, _, length_z = linear_ref.shape
    rows = planes_ref.shape[0]
    pitch = channels + 8
    pack = 2 * M * M // rows
    group = lax.broadcasted_iota(jnp.int32, (16, 256), 1) // M % 8
    keeps = []
    for step in range(4):
        keep = jnp.where(group // 2 == step, 1.0, 0.0).astype(BF16)
        keeps.append(jnp.concatenate([keep] * (channels // 16), axis=0))
    lane = lax.broadcasted_iota(jnp.int32, (M, 128), 1)

    def block(index):
        return planes_ref[index * M : (index + 1) * M, :]

    def halves(turned):
        found = []
        for low_bit in range(pack):
            first = low_bit * 2 * channels
            found.append(
                jnp.concatenate(
                    [turned[first : first + channels], turned[first + channels : first + 2 * channels]], axis=1
                )
            )
        return found

    def along_z(parts, which, steps):
        terms = [split(part) for part in parts]
        left = []
        for step in steps:
            for high, low in terms:
                high, low = high * keeps[step], low * keeps[step]
                left.append(jnp.concatenate([high, low, high], axis=1))
        right = jnp.concatenate([iz_ref[which, 0], iz_ref[which, 0], iz_ref[which, 1]], axis=0)
        return dot(jnp.concatenate(left, axis=0), right)

    def put(value, part, k):
        first = mode_row(part, k) * pitch
        rows_ref[first : first + channels, :] = value

    blocks = rows // M
    octets = blocks // 16
    for octet in range(octets):
        sums, differences = [], []
        for place in range(8):
            index = octet * 8 + place
            plus = block(index)
            minus = block(blocks - index) if index > 0 else jnp.zeros_like(plus)
            if pack == 2:
                minus = jnp.where(lane < 64, minus, block(blocks - 1 - index))
            sums.append(plus + minus)
            differences.append(plus - minus)
        for part, stack in enumerate((sums, differences)):
            parts = halves(jnp.concatenate(stack, axis=0).T)
            value = along_z(parts, part, range(4))
            for step in range(4):
                for low_bit in range(pack):
                    first = (step * pack + low_bit) * channels
                    for parity in range(2):
                        k = (octet * 8 + step * 2 + parity) * pack + low_bit
                        put(
                            value[first : first + channels, parity * length_z : (parity + 1) * length_z],
                            part,
                            k,
                        )
    last = block(blocks // 2)
    last = jnp.concatenate([last, jnp.zeros((128 - M, 128), F32)], axis=0).T
    first_half = halves(last)[:1]
    put(along_z(first_half, 0, [0])[:, :length_z], 0, M)
    put(-along_z(first_half, 1, [0])[:, :length_z], 1, M)
    rows_ref[(2 * M + 2) * pitch :, :] = jnp.zeros(((ROWS - 2 * M - 2) * pitch, length_z), F32)
    copies = []
    for pair in range(channels // 2):
        columns = [rows_ref[pl.ds(2 * pair + side, ROWS, stride=pitch), :] for side in range(2)]
        high, low = split(jnp.concatenate(columns, axis=1))
        value = dot(iy_ref[...], jnp.concatenate([high, low, high], axis=0))
        for side in range(2):
            channel = 2 * pair + side
            spectral = value[:, side * length_z : (side + 1) * length_z]
            out_ref[channel] = (spectral + linear_ref[channel]).astype(BF16)
        if pair % 4 == 3:
            part = pl.ds(2 * pair - 6, 8)
            copies.append(pltpu.make_async_copy(out_ref.at[part], out_hbm.at[part], sems.at[len(copies)]))
            copies[-1].start()
    for copy in copies:
        copy.wait()


def in_hbm(value):
    return pltpu.with_memory_space_constraint(value, pltpu.HBM)


def call(kernel, out_shape, scratch, limit, flops, moved, *args, **kwargs):
    return pl.pallas_call(
        kernel,
        out_shape=out_shape,
        **kwargs,
        scratch_shapes=scratch,
        compiler_params=pltpu.CompilerParams(vmem_limit_bytes=limit * MIB),
        cost_estimate=pl.CostEstimate(flops=flops, bytes_accessed=moved, transcendentals=0),
    )(*args)


def weight_terms(modes, channels):
    parts = modes.reshape(modes.shape[:3] + (2, 2, channels))
    in_real, in_imag = parts[..., 0, 0, :, None], parts[..., 1, 0, :, None]
    cot_real, cot_imag = parts[..., 0, 1, None, :], parts[..., 1, 1, None, :]
    real = jnp.sum(in_real * cot_real + in_imag * cot_imag, axis=0)
    imag = jnp.sum(in_real * cot_imag - in_imag * cot_real, axis=0)
    stacked = jnp.stack([real, imag], axis=2)
    return stacked.reshape(stacked.shape[:2] + (-1,))


def on_device(field, cotangent, spectral_weight, pointwise_weight):
    _, planes, channels, length_y, length_z = field.shape
    pairs, kept_x, _ = spectral_weight.shape
    groups = lax.axis_size("gx")
    samples = lax.axis_size("dp")
    width_x = planes * groups
    share = kept_x // samples
    pack = 2 if pairs == 2 * M else 1
    count = pairs // pack
    all_pairs = 2 * M * M
    cells = width_x * length_y * length_z
    shape = jax.ShapeDtypeStruct
    field = field.reshape(channels, length_y, length_z)
    cotangent = cotangent.reshape(channels, length_y, length_z)

    fy, fz = forward_tables(length_y, length_z)
    iz, iy = inverse_tables(length_y, length_z)
    fx, ix = x_tables(kept_x, width_x)
    scale = np.where(np.arange(M) == 0, 1.0, 2.0) / cells
    scale = np.tile(scale, 8).astype(np.float32)[None]

    hbm = pl.BlockSpec(memory_space=pltpu.HBM)
    spectra = call(
        forward_kernel,
        pltpu.VMEM((all_pairs, 128), F32),
        [
            pltpu.VMEM((2,) + field.shape, BF16),
            pltpu.VMEM(scale.shape, F32),
            pltpu.VMEM(fy.shape, BF16),
            pltpu.VMEM(fz.shape, BF16),
            pltpu.VMEM((8, 2 * length_z, 256), BF16),
            pltpu.VMEM((2 * channels * PITCH, length_z), F32),
            pltpu.SemaphoreType.DMA((7,)),
        ],
        16, 10**9, 5 * 10**6,
        *[in_hbm(one) for one in (field, cotangent, scale, fy, fz)],
        in_specs=[hbm] * 5,
    )
    spectra, spectral_weight, spread, gather = lax.optimization_barrier(
        (spectra, spectral_weight, spread_table(channels), gather_table(channels))
    )
    received = lax.all_to_all(
        spectra.reshape(groups, pairs, 128), "gx", split_axis=0, concat_axis=0, tiled=True
    )
    mine, other, grads = call(
        functools.partial(mid_kernel, samples),
        (
            pltpu.VMEM((pairs, share, 128), F32),
            pltpu.VMEM((pairs * (samples - 1), share, 128), F32),
            pltpu.VMEM((width_x * count, 128), F32),
        ),
        [
            pltpu.VMEM((pairs * kept_x, 128), F32),
            pltpu.VMEM((2 * pairs * kept_x, gather.shape[0]), BF16),
        ],
        16, 10**9, 4 * 10**6,
        received.reshape(width_x * pairs, 128), spectral_weight, fx, ix, spread, gather,
    )
    returned = lax.all_to_all(
        grads.reshape(groups, count, 128), "gx", split_axis=0, concat_axis=0, tiled=True
    )
    split_samples = samples == 2 and share % 8 == 0
    kept = [mine, repeat_table(channels)] if split_samples else []
    tall = (pairs, share, 2 * channels * channels)
    _, late = lax.optimization_barrier((grads, cotangent))
    linear, *weight_grad = call(
        functools.partial(local_kernel, len(kept)),
        [shape((channels, length_y, length_z), F32)] + [shape(tall, F32)] * (len(kept) // 2),
        [
            pltpu.VMEM((channels, length_y, length_z), BF16),
            pltpu.VMEM((16 * channels, 16 * channels), BF16),
            pltpu.SemaphoreType.DMA(()),
        ],
        16, 4 * 10**9, 5 * 10**6,
        in_hbm(late), pointwise_weight, *kept,
        in_specs=[hbm] + [pl.BlockSpec()] * (1 + len(kept)),
    )
    if split_samples:
        other = lax.ppermute(other, "dp", [(0, 1), (1, 0)])
        weight_grad = call(
            weight_kernel,
            shape(tall, F32),
            [pltpu.VMEM(tall, F32), pltpu.SemaphoreType.DMA((4,))],
            16, 2 * 10**9, 5 * 10**6,
            other, kept[1], *weight_grad,
            out_specs=hbm,
        )
    else:
        me = lax.axis_index("dp")
        modes = jnp.concatenate([mine[None], other.reshape(samples - 1, pairs, share, 128)])
        modes = jnp.roll(modes, me, 0)
        modes = lax.all_to_all(modes, "dp", split_axis=0, concat_axis=0, tiled=True)
        weight_grad = weight_terms(modes, channels)
    field_grad = call(
        inverse_kernel,
        shape((channels, length_y, length_z), BF16),
        [
            pltpu.VMEM((ROWS * (channels + 8), length_z), F32),
            pltpu.VMEM((channels, length_y, length_z), BF16),
            pltpu.SemaphoreType.DMA((channels // 8,)),
        ],
        16, 10**9, 4 * 10**6,
        returned.reshape(width_x * count, 128), linear, iz, iy,
        out_specs=hbm,
    )
    return field_grad.reshape(1, planes, channels, length_y, length_z), weight_grad


def solution(mesh):
    placed = (
        P("dp", "gx", None, None, None),
        P("dp", "gx", None, None, None),
        P("gx", None, None),
        P(),
    )
    return jax.shard_map(
        on_device,
        mesh=mesh,
        in_specs=placed,
        out_specs=(P("dp", "gx", None, None, None), P("gx", "dp", None)),
        check_vma=False,
    )
```

```python
import functools
import math

import jax
import jax.numpy as jnp
import ml_dtypes
import numpy as np
from jax import lax
from jax.experimental import pallas as pl
from jax.experimental.pallas import tpu as pltpu
from jax.sharding import PartitionSpec as P

M = 16
F32 = jnp.float32
BF16 = jnp.bfloat16
MIB = 1024 * 1024
ROWS = 3 * M
PITCH = ROWS - 8


def kept_freqs(half_count, length):
    index = np.arange(2 * half_count)
    return np.where(index < half_count, index, index + length - 2 * half_count)


def phases(frequency, length):
    product = np.outer(frequency, np.arange(length)) % length
    angle = product * (2.0 * math.pi / length)
    return np.cos(angle), np.sin(angle)


def split_np(table):
    high = table.astype(ml_dtypes.bfloat16)
    low = (table - high.astype(np.float64)).astype(ml_dtypes.bfloat16)
    return high, low


def split(value):
    high = value.astype(BF16)
    low = (value - high.astype(F32)).astype(BF16)
    return high, low


def dot(left, right):
    return jnp.dot(left, right, preferred_element_type=F32)


def forward_tables(length_y, length_z):
    cos_y, sin_y = phases(np.arange(M + 1), length_y)
    rows = np.zeros((ROWS, length_y))
    rows[:M], rows[M : 2 * M] = cos_y[:M], -sin_y[:M]
    rows[2 * M], rows[2 * M + 1] = cos_y[M], -sin_y[M]
    along_y = np.concatenate(split_np(rows), 1)
    cos_z, sin_z = phases(np.arange(M), length_z)
    along_z = np.concatenate([np.tile(cos_z.T, (1, 8)), np.tile(sin_z.T, (1, 8))], 1)
    return np.concatenate((along_y,) + split_np(along_z))


def inverse_tables(length_y, length_z):
    cos_z, sin_z = phases(np.arange(M), length_z)
    along_z = np.zeros((2, 2, 8, M, 2, length_z))
    for place in range(8):
        along_z[0, 0, place, :, place % 2] = cos_z
        along_z[0, 1, place, :, place % 2] = -sin_z
        along_z[1, 0, place, :, place % 2] = sin_z
        along_z[1, 1, place, :, place % 2] = cos_z
    along_z = along_z.reshape(2, 2 * 8 * M, 2 * length_z)
    along_z = np.stack([np.stack(split_np(part)) for part in along_z])
    cos_y, sin_y = phases(np.arange(M + 1), length_y)
    columns = np.zeros((length_y, ROWS))
    for k in range(M + 1):
        columns[:, mode_row(0, k)] = cos_y[k]
        columns[:, mode_row(1, k)] = -sin_y[k]
    high, low = split_np(columns)
    return along_z, np.concatenate([high, high, low], 1)


def mode_row(part, k):
    return 2 * M + part if k == M else part * M + k


def x_tables(kept_x, width_x):
    cos_x, sin_x = phases(kept_freqs(kept_x // 2, width_x), width_x)
    high, low = split_np(np.concatenate([cos_x, sin_x], 1))
    forward = np.concatenate([high, high, low], 1)
    high, low = split_np(np.concatenate([cos_x.T, sin_x.T], 1))
    inverse = np.concatenate([high, high, low], 1)
    return forward, inverse


def spread_table(channels):
    copies = 128 // channels
    table = np.zeros((2, 2, 2, channels, 2, copies, channels))
    eye = np.eye(channels)
    for part in range(2):
        table[:, part, 1, :, part] = eye[:, None, :]
    return table.reshape(8 * channels, 256).astype(ml_dtypes.bfloat16)


LEVELS = 1


def gather_table(channels):
    width = channels * channels >> LEVELS
    place = np.arange(width)
    block, lane = place // 128, place % 128
    step = block << LEVELS
    for level in range(LEVELS):
        step = step + ((lane & 16 >> level) > 0) * (1 << level)
    i = step * (128 // channels) + lane // channels
    table = np.zeros((2, width, 2, 2, 2, channels))
    for part in range(2):
        table[part, place, 0, :, part, i] = 1.0
        table[part, place, 1, :, 1 - part, i] = 1.0 - 2.0 * part
    return table.reshape(2 * width, 8 * channels).astype(ml_dtypes.bfloat16)


def repeat_table(channels):
    square = channels * channels
    table = np.zeros((2, 2, channels, 2 * square + 256))
    for i in range(channels):
        for part in range(2):
            start = part * square + i * channels
            table[part, 0, i, start : start + channels] = 1.0
            table[part, 1, i, 2 * square + part * 128 + i : 2 * square + part * 128 + 128 : channels] = 1.0
    return table.reshape(4 * channels, -1).astype(ml_dtypes.bfloat16)


def forward_kernel(
    cells, field_hbm, cot_hbm, table_hbm, out_ref, data_ref, table_ref, spread_ref, rows_ref, sems
):
    channels, length_y, length_z = field_hbm.shape
    copies = []

    def start(source, target):
        copy = pltpu.make_async_copy(source, target, sems.at[len(copies)])
        copy.start()
        copies.append(copy)
        return copy

    table = start(table_hbm, table_ref)
    chunks = [start(ref, data_ref.at[array]) for array, ref in enumerate((field_hbm, cot_hbm))]
    table.wait()
    along_y = jnp.concatenate([table_ref[:ROWS, :length_y], table_ref[:ROWS, length_y:]], axis=0)
    group = lax.broadcasted_iota(jnp.int32, (16, 256), 1) // M % 8
    for place in range(8):
        keep = jnp.where(group == place, 1.0, 0.0).astype(BF16)
        keep = jnp.concatenate([keep] * (length_z // 16), axis=0)
        for term in range(2):
            first = ROWS + term * length_z
            spread_ref[place, term * length_z : (term + 1) * length_z, :] = (
                table_ref[first : first + length_z, :] * keep
            )
    for array, copy in enumerate(chunks):
        copy.wait()
        for pair in range(channels // 2):
            data = jnp.concatenate([data_ref[array, 2 * pair], data_ref[array, 2 * pair + 1]], axis=1)
            both = dot(along_y, data)
            value = both[:PITCH] + both[ROWS : ROWS + PITCH]
            base = (array * channels + 2 * pair) * PITCH
            rows_ref[base : base + PITCH, :] = value[:, :length_z]
            rows_ref[base + PITCH : base + 2 * PITCH, :] = value[:, length_z:]
    kz = lax.broadcasted_iota(jnp.int32, (1, 128), 1) % M
    scale = jnp.where(kz == 0, 1.0 / cells, 2.0 / cells).astype(F32)
    count = 2 * channels
    lefts, rights = [], []
    for place in range(8):
        table_high, table_low = spread_ref[place, :length_z], spread_ref[place, length_z:]
        sources = [part * M + octet * 8 + place for part in range(2) for octet in range(2)]
        if place == 0:
            sources += [2 * M, 2 * M + 1]
        rows = [rows_ref[pl.ds(source, count, stride=PITCH), :] for source in sources]
        high, low = split(jnp.concatenate(rows, axis=0))
        left = jnp.concatenate([high, low, high], axis=1)
        right = jnp.concatenate([table_high, table_high, table_low], axis=0)
        if place == 0:
            last = dot(left[4 * count :], right)
            left = left[: 4 * count]
        lefts.append(left)
        rights.append(right)
    total = dot(jnp.concatenate(lefts, axis=1), jnp.concatenate(rights, axis=0))

    def turned(real, imag, sign):
        if sign > 0:
            block = (real[:, :128] + imag[:, 128:], imag[:, :128] - real[:, 128:])
        else:
            block = (real[:, :128] - imag[:, 128:], -imag[:, :128] - real[:, 128:])
        scaled = []
        for part in block:
            scaled += [part[:channels], part[channels:] * scale]
        return jnp.concatenate(scaled, axis=0).T

    for octet in range(2):
        real = total[octet * count : (octet + 1) * count]
        imag = total[(2 + octet) * count : (3 + octet) * count]
        out_ref[octet * 128 : (octet + 1) * 128, :] = turned(real, imag, 1)
        minus = turned(real, imag, -1)
        for place in range(8):
            k = octet * 8 + place
            if k > 0:
                out_ref[(2 * M - k) * M : (2 * M - k + 1) * M, :] = minus[place * M : (place + 1) * M]
    out_ref[M * M : (M + 1) * M, :] = turned(last[:count], last[count:], -1)[:M]


def mid_kernel(
    samples, planes_ref, weight_ref, fx_ref, ix_ref, spread_ref, gather_ref,
    mine_ref, other_ref, out_ref, rows_ref, split_ref,
):
    pairs, kept_x, _ = weight_ref.shape
    width_x = planes_ref.shape[0] // pairs
    pack = width_x * pairs // out_ref.shape[0]
    share = kept_x // samples
    me = lax.axis_index("dp")
    lane = lax.broadcasted_iota(jnp.int32, (width_x, 128), 1)
    sign = jnp.where(lane < 64, 1.0, -1.0).astype(F32)
    for step in range(pairs // 2):
        columns = []
        for q in (2 * step, 2 * step + 1):
            plane = planes_ref[pl.ds(q, width_x, stride=pairs), :]
            turned = pltpu.roll(plane, 64, 1) * sign
            columns.append(jnp.concatenate([plane, turned], axis=0))
        high, low = split(jnp.concatenate(columns, axis=1))
        modes = dot(fx_ref[...], jnp.concatenate([high, low, high], axis=0))
        for index, q in enumerate((2 * step, 2 * step + 1)):
            mode = modes[:, index * 128 : (index + 1) * 128]
            rows_ref[q * kept_x : (q + 1) * kept_x, :] = mode
    for q in range(pairs):
        for ahead in range(samples):
            start = q * kept_x + lax.rem(me + ahead, samples) * share
            part = rows_ref[pl.ds(pl.multiple_of(start, share), share), :]
            if ahead == 0:
                mine_ref[q] = part
            else:
                other_ref[(ahead - 1) * pairs + q] = part

    square = weight_ref.shape[2] // 2
    width = square >> LEVELS
    lane = lax.broadcasted_iota(jnp.int32, (kept_x, 128), 1)

    def merge(one, two, shift):
        first = lane & shift == 0
        moved = jnp.where(first, two, one)
        moved = jnp.take_along_axis(moved, lane ^ shift, axis=1, mode="promise_in_bounds")
        return jnp.where(first, one, two) + moved

    def products(rows, q, start):
        real, imag = rows[:, :128], rows[:, 128:]
        w_real = weight_ref[q, :, start : start + 128].astype(F32)
        w_imag = weight_ref[q, :, square + start : square + start + 128].astype(F32)
        return real * w_real + imag * w_imag, imag * w_real - real * w_imag

    grads = []
    chunk = 8
    for first in range(0, pairs, chunk):
        high, low = split(rows_ref[first * kept_x : (first + chunk) * kept_x, :])
        spread = dot(jnp.concatenate([high, low], axis=1), spread_ref[...])
        size = chunk * kept_x
        base = 2 * first * kept_x
        for place in range(chunk):
            rows = spread[place * kept_x : (place + 1) * kept_x]
            at = base + place * kept_x
            for column in range(0, width, 128):
                items = [
                    products(rows, first + place, start)
                    for start in range(column << LEVELS, column + 128 << LEVELS, 128)
                ]
                for part in range(2):
                    values = [item[part] for item in items]
                    for level in range(LEVELS):
                        values = [merge(one, two, 16 >> level) for one, two in zip(values[::2], values[1::2])]
                    high, low = split(values[0])
                    at_column = part * width + column
                    split_ref[at : at + kept_x, at_column : at_column + 128] = high
                    split_ref[at + size : at + size + kept_x, at_column : at_column + 128] = low
        both = dot(split_ref[base : base + 2 * size, :], gather_ref[...])
        grads.append(both[:size] + both[size:])
    grads = jnp.concatenate(grads, axis=0)
    count = pairs // pack
    if pack == 2:
        size = count * kept_x
        lane = lax.broadcasted_iota(jnp.int32, (size, 256), 1) % 128
        grads = jnp.where(lane < 64, grads[:size], grads[size:])
    for step in range(count // 2):
        columns = []
        for row in (2 * step, 2 * step + 1):
            block = grads[row * kept_x : (row + 1) * kept_x]
            columns.append(jnp.concatenate([block[:, :128], block[:, 128:]], axis=0))
        high, low = split(jnp.concatenate(columns, axis=1))
        planes = dot(ix_ref[...], jnp.concatenate([high, low, high], axis=0))
        for index, row in enumerate((2 * step, 2 * step + 1)):
            out_ref[pl.ds(row, width_x, stride=count), :] = planes[:, index * 128 : (index + 1) * 128]


def weight_terms_in(modes_ref, repeat_ref, part, emit):
    square = (repeat_ref.shape[1] - 256) // 2
    rows = modes_ref[part]
    shape = rows.shape[:2] + (256,)
    high, low = split(rows.reshape(shape[0] * shape[1], 128))
    side = jnp.concatenate([high, low], axis=1)

    def repeated(start):
        table = repeat_ref[:, start : start + 256]
        return dot(side, jnp.concatenate([table, table], axis=0))

    cots = repeated(2 * square)
    c_real = jnp.concatenate([cots[:, :128]] * 2, axis=1)
    c_imag = jnp.concatenate([cots[:, 128:]] * 2, axis=1)
    for start in range(0, square, 256):
        f_real, f_imag = repeated(start), repeated(square + start)
        emit(start, (f_real * c_real + f_imag * c_imag).reshape(shape))
        emit(square + start, (f_real * c_imag - f_imag * c_real).reshape(shape))


def weight_kernel(modes_ref, repeat_ref, before_ref, out_hbm, out_ref, sems):
    pairs = modes_ref.shape[0]
    copies = []
    for first in range(0, pairs, pairs // 4):
        part = pl.ds(first, pairs // 4)

        def emit(start, value):
            out_ref[part, :, start : start + 256] = before_ref[part, :, start : start + 256] + value

        weight_terms_in(modes_ref, repeat_ref, part, emit)
        copies.append(pltpu.make_async_copy(out_ref.at[part], out_hbm.at[part], sems.at[len(copies)]))
        copies[-1].start()
    for copy in copies:
        copy.wait()


def local_kernel(kept, *refs):
    cot_hbm, weight_ref = refs[:2]
    linear_ref, cot_ref, mix_ref, sem = refs[kept + 2], *refs[-3:]
    copy = pltpu.make_async_copy(cot_hbm, cot_ref, sem)
    copy.start()
    if kept:
        modes_ref, repeat_ref, out_ref = refs[2], refs[3], refs[5]
        pairs = modes_ref.shape[0]
        for first in range(0, pairs, pairs // 4):
            part = pl.ds(first, pairs // 4)

            def emit(start, value):
                out_ref[part, :, start : start + 256] = value

            weight_terms_in(modes_ref, repeat_ref, part, emit)
    channels, length_y, length_z = cot_ref.shape
    size = 16 * channels
    left = lax.broadcasted_iota(jnp.int32, (size, channels), 0) // 16 == lax.broadcasted_iota(
        jnp.int32, (size, channels), 1
    )
    right = lax.broadcasted_iota(jnp.int32, (channels, size), 1) // 16 == lax.broadcasted_iota(
        jnp.int32, (channels, size), 0
    )
    tall = dot(left.astype(F32).astype(BF16), weight_ref[...]).astype(BF16)
    wide = dot(tall, right.astype(F32).astype(BF16))
    same = lax.broadcasted_iota(jnp.int32, (size, size), 0) % 16 == lax.broadcasted_iota(
        jnp.int32, (size, size), 1
    ) % 16
    mix_ref[...] = jnp.where(same, wide, 0.0).astype(BF16)
    copy.wait()
    for step in range(length_y // 32):
        columns = []
        for part in range(2):
            first = step * 32 + part * 16
            columns.append(cot_ref[:, first : first + 16, :].reshape(channels * 16, length_z))
        mixed = dot(mix_ref[...], jnp.concatenate(columns, axis=1))
        for part in range(2):
            first = step * 32 + part * 16
            linear_ref[:, first : first + 16, :] = mixed[:, part * length_z : (part + 1) * length_z].reshape(
                channels, 16, length_z
            )


def inverse_kernel(planes_ref, linear_ref, iz_ref, iy_ref, out_hbm, rows_ref, out_ref, sems):
    channels, _, length_z = linear_ref.shape
    rows = planes_ref.shape[0]
    pitch = channels + 8
    pack = 2 * M * M // rows
    group = lax.broadcasted_iota(jnp.int32, (16, 256), 1) // M % 8
    keeps = []
    for step in range(4):
        keep = jnp.where(group // 2 == step, 1.0, 0.0).astype(BF16)
        keeps.append(jnp.concatenate([keep] * (channels // 16), axis=0))
    lane = lax.broadcasted_iota(jnp.int32, (M, 128), 1)

    def block(index):
        return planes_ref[index * M : (index + 1) * M, :]

    def halves(turned):
        found = []
        for low_bit in range(pack):
            first = low_bit * 2 * channels
            found.append(
                jnp.concatenate(
                    [turned[first : first + channels], turned[first + channels : first + 2 * channels]], axis=1
                )
            )
        return found

    def along_z(parts, which, steps):
        terms = [split(part) for part in parts]
        left = []
        for step in steps:
            for high, low in terms:
                high, low = high * keeps[step], low * keeps[step]
                left.append(jnp.concatenate([high, low, high], axis=1))
        right = jnp.concatenate([iz_ref[which, 0], iz_ref[which, 0], iz_ref[which, 1]], axis=0)
        return dot(jnp.concatenate(left, axis=0), right)

    def put(value, part, k):
        first = mode_row(part, k) * pitch
        rows_ref[first : first + channels, :] = value

    blocks = rows // M
    octets = blocks // 16
    for octet in range(octets):
        sums, differences = [], []
        for place in range(8):
            index = octet * 8 + place
            plus = block(index)
            minus = block(blocks - index) if index > 0 else jnp.zeros_like(plus)
            if pack == 2:
                minus = jnp.where(lane < 64, minus, block(blocks - 1 - index))
            sums.append(plus + minus)
            differences.append(plus - minus)
        for part, stack in enumerate((sums, differences)):
            parts = halves(jnp.concatenate(stack, axis=0).T)
            value = along_z(parts, part, range(4))
            for step in range(4):
                for low_bit in range(pack):
                    first = (step * pack + low_bit) * channels
                    for parity in range(2):
                        k = (octet * 8 + step * 2 + parity) * pack + low_bit
                        put(
                            value[first : first + channels, parity * length_z : (parity + 1) * length_z],
                            part,
                            k,
                        )
    last = block(blocks // 2)
    last = jnp.concatenate([last, jnp.zeros((128 - M, 128), F32)], axis=0).T
    first_half = halves(last)[:1]
    put(along_z(first_half, 0, [0])[:, :length_z], 0, M)
    put(-along_z(first_half, 1, [0])[:, :length_z], 1, M)
    rows_ref[(2 * M + 2) * pitch :, :] = jnp.zeros(((ROWS - 2 * M - 2) * pitch, length_z), F32)
    copies = []
    for pair in range(channels // 2):
        columns = [rows_ref[pl.ds(2 * pair + side, ROWS, stride=pitch), :] for side in range(2)]
        high, low = split(jnp.concatenate(columns, axis=1))
        value = dot(iy_ref[...], jnp.concatenate([high, low, high], axis=0))
        for side in range(2):
            channel = 2 * pair + side
            spectral = value[:, side * length_z : (side + 1) * length_z]
            out_ref[channel] = (spectral + linear_ref[channel]).astype(BF16)
        if pair % 4 == 3:
            part = pl.ds(2 * pair - 6, 8)
            copies.append(pltpu.make_async_copy(out_ref.at[part], out_hbm.at[part], sems.at[len(copies)]))
            copies[-1].start()
    for copy in copies:
        copy.wait()


def in_hbm(value):
    return pltpu.with_memory_space_constraint(value, pltpu.HBM)


def call(kernel, out_shape, scratch, limit, flops, moved, *args, **kwargs):
    return pl.pallas_call(
        kernel,
        out_shape=out_shape,
        **kwargs,
        scratch_shapes=scratch,
        compiler_params=pltpu.CompilerParams(vmem_limit_bytes=limit * MIB),
        cost_estimate=pl.CostEstimate(flops=flops, bytes_accessed=moved, transcendentals=0),
    )(*args)


def weight_terms(modes, channels):
    parts = modes.reshape(modes.shape[:3] + (2, 2, channels))
    in_real, in_imag = parts[..., 0, 0, :, None], parts[..., 1, 0, :, None]
    cot_real, cot_imag = parts[..., 0, 1, None, :], parts[..., 1, 1, None, :]
    real = jnp.sum(in_real * cot_real + in_imag * cot_imag, axis=0)
    imag = jnp.sum(in_real * cot_imag - in_imag * cot_real, axis=0)
    stacked = jnp.stack([real, imag], axis=2)
    return stacked.reshape(stacked.shape[:2] + (-1,))


def on_device(field, cotangent, spectral_weight, pointwise_weight):
    _, planes, channels, length_y, length_z = field.shape
    pairs, kept_x, _ = spectral_weight.shape
    groups = lax.axis_size("gx")
    samples = lax.axis_size("dp")
    width_x = planes * groups
    share = kept_x // samples
    pack = 2 if pairs == 2 * M else 1
    count = pairs // pack
    all_pairs = 2 * M * M
    cells = width_x * length_y * length_z
    shape = jax.ShapeDtypeStruct
    field = field.reshape(channels, length_y, length_z)
    cotangent = cotangent.reshape(channels, length_y, length_z)

    forward = forward_tables(length_y, length_z)
    iz, iy = inverse_tables(length_y, length_z)
    fx, ix = x_tables(kept_x, width_x)
    hbm = pl.BlockSpec(memory_space=pltpu.HBM)
    spectra = call(
        functools.partial(forward_kernel, cells),
        pltpu.VMEM((all_pairs, 128), F32),
        [
            pltpu.VMEM((2,) + field.shape, BF16),
            pltpu.VMEM(forward.shape, BF16),
            pltpu.VMEM((8, 2 * length_z, 256), BF16),
            pltpu.VMEM((2 * channels * PITCH, length_z), F32),
            pltpu.SemaphoreType.DMA((3,)),
        ],
        16, 10**9, 5 * 10**6,
        *[in_hbm(one) for one in (field, cotangent, forward)],
        in_specs=[hbm] * 3,
    )
    spectra, spectral_weight, spread, gather = lax.optimization_barrier(
        (spectra, spectral_weight, spread_table(channels), gather_table(channels))
    )
    received = lax.all_to_all(
        spectra.reshape(groups, pairs, 128), "gx", split_axis=0, concat_axis=0, tiled=True
    )
    mine, other, grads = call(
        functools.partial(mid_kernel, samples),
        (
            pltpu.VMEM((pairs, share, 128), F32),
            pltpu.VMEM((pairs * (samples - 1), share, 128), F32),
            pltpu.VMEM((width_x * count, 128), F32),
        ),
        [
            pltpu.VMEM((pairs * kept_x, 128), F32),
            pltpu.VMEM((2 * pairs * kept_x, gather.shape[0]), BF16),
        ],
        16, 10**9, 4 * 10**6,
        received.reshape(width_x * pairs, 128), spectral_weight, fx, ix, spread, gather,
    )
    returned = lax.all_to_all(
        grads.reshape(groups, count, 128), "gx", split_axis=0, concat_axis=0, tiled=True
    )
    split_samples = samples == 2 and share % 8 == 0
    kept = [mine, repeat_table(channels)] if split_samples else []
    tall = (pairs, share, 2 * channels * channels)
    _, late = lax.optimization_barrier((grads, cotangent))
    linear, *weight_grad = call(
        functools.partial(local_kernel, len(kept)),
        [shape((channels, length_y, length_z), F32)] + [shape(tall, F32)] * (len(kept) // 2),
        [
            pltpu.VMEM((channels, length_y, length_z), BF16),
            pltpu.VMEM((16 * channels, 16 * channels), BF16),
            pltpu.SemaphoreType.DMA(()),
        ],
        16, 4 * 10**9, 5 * 10**6,
        in_hbm(late), pointwise_weight, *kept,
        in_specs=[hbm] + [pl.BlockSpec()] * (1 + len(kept)),
    )
    if split_samples:
        other = lax.ppermute(other, "dp", [(0, 1), (1, 0)])
        weight_grad = call(
            weight_kernel,
            shape(tall, F32),
            [pltpu.VMEM(tall, F32), pltpu.SemaphoreType.DMA((4,))],
            16, 2 * 10**9, 5 * 10**6,
            other, kept[1], *weight_grad,
            out_specs=hbm,
        )
    else:
        me = lax.axis_index("dp")
        modes = jnp.concatenate([mine[None], other.reshape(samples - 1, pairs, share, 128)])
        modes = jnp.roll(modes, me, 0)
        modes = lax.all_to_all(modes, "dp", split_axis=0, concat_axis=0, tiled=True)
        weight_grad = weight_terms(modes, channels)
    field_grad = call(
        inverse_kernel,
        shape((channels, length_y, length_z), BF16),
        [
            pltpu.VMEM((ROWS * (channels + 8), length_z), F32),
            pltpu.VMEM((channels, length_y, length_z), BF16),
            pltpu.SemaphoreType.DMA((channels // 8,)),
        ],
        16, 10**9, 4 * 10**6,
        returned.reshape(width_x * count, 128), linear, iz, iy,
        out_specs=hbm,
    )
    return field_grad.reshape(1, planes, channels, length_y, length_z), weight_grad


def solution(mesh):
    placed = (
        P("dp", "gx", None, None, None),
        P("dp", "gx", None, None, None),
        P("gx", None, None),
        P(),
    )
    return jax.shard_map(
        on_device,
        mesh=mesh,
        in_specs=placed,
        out_specs=(P("dp", "gx", None, None, None), P("gx", "dp", None)),
        check_vma=False,
    )
```

```python
import functools
import math

import jax
import jax.numpy as jnp
import ml_dtypes
import numpy as np
from jax import lax
from jax.experimental import pallas as pl
from jax.experimental.pallas import tpu as pltpu
from jax.sharding import PartitionSpec as P

M = 16
F32 = jnp.float32
BF16 = jnp.bfloat16
MIB = 1024 * 1024
ROWS = 3 * M
PITCH = ROWS - 8


def kept_freqs(half_count, length):
    index = np.arange(2 * half_count)
    return np.where(index < half_count, index, index + length - 2 * half_count)


def phases(frequency, length):
    product = np.outer(frequency, np.arange(length)) % length
    angle = product * (2.0 * math.pi / length)
    return np.cos(angle), np.sin(angle)


def split_np(table):
    high = table.astype(ml_dtypes.bfloat16)
    low = (table - high.astype(np.float64)).astype(ml_dtypes.bfloat16)
    return high, low


def split(value):
    high = value.astype(BF16)
    low = (value - high.astype(F32)).astype(BF16)
    return high, low


def dot(left, right):
    return jnp.dot(left, right, preferred_element_type=F32)


def forward_tables(length_y, length_z):
    cos_y, sin_y = phases(np.arange(M + 1), length_y)
    rows = np.zeros((ROWS, length_y))
    rows[:M], rows[M : 2 * M] = cos_y[:M], -sin_y[:M]
    rows[2 * M], rows[2 * M + 1] = cos_y[M], -sin_y[M]
    along_y = np.concatenate(split_np(rows), 1)
    cos_z, sin_z = phases(np.arange(M), length_z)
    along_z = np.concatenate([np.tile(cos_z.T, (1, 8)), np.tile(sin_z.T, (1, 8))], 1)
    return np.concatenate((along_y,) + split_np(along_z))


def inverse_tables(length_y, length_z):
    cos_z, sin_z = phases(np.arange(M), length_z)
    along_z = np.zeros((2, 2, 8, M, 2, length_z))
    for place in range(8):
        along_z[0, 0, place, :, place % 2] = cos_z
        along_z[0, 1, place, :, place % 2] = -sin_z
        along_z[1, 0, place, :, place % 2] = sin_z
        along_z[1, 1, place, :, place % 2] = cos_z
    along_z = along_z.reshape(2, 2 * 8 * M, 2 * length_z)
    along_z = np.stack([np.stack(split_np(part)) for part in along_z])
    cos_y, sin_y = phases(np.arange(M + 1), length_y)
    columns = np.zeros((length_y, ROWS))
    for k in range(M + 1):
        columns[:, mode_row(0, k)] = cos_y[k]
        columns[:, mode_row(1, k)] = -sin_y[k]
    high, low = split_np(columns)
    return along_z, np.concatenate([high, high, low], 1)


def mode_row(part, k):
    return 2 * M + part if k == M else part * M + k


def x_tables(kept_x, width_x):
    cos_x, sin_x = phases(kept_freqs(kept_x // 2, width_x), width_x)
    high, low = split_np(np.concatenate([cos_x, sin_x], 1))
    forward = np.concatenate([high, high, low], 1)
    high, low = split_np(np.concatenate([cos_x.T, sin_x.T], 1))
    inverse = np.concatenate([high, high, low], 1)
    return forward, inverse


def spread_table(channels):
    copies = 128 // channels
    table = np.zeros((2, 2, 2, channels, 2, copies, channels))
    eye = np.eye(channels)
    for part in range(2):
        table[:, part, 1, :, part] = eye[:, None, :]
    return table.reshape(8 * channels, 256).astype(ml_dtypes.bfloat16)


LEVELS = 1


def gather_table(channels):
    width = channels * channels >> LEVELS
    place = np.arange(width)
    block, lane = place // 128, place % 128
    step = block << LEVELS
    for level in range(LEVELS):
        step = step + ((lane & 16 >> level) > 0) * (1 << level)
    i = step * (128 // channels) + lane // channels
    table = np.zeros((2, width, 2, 2, 2, channels))
    for part in range(2):
        table[part, place, 0, :, part, i] = 1.0
        table[part, place, 1, :, 1 - part, i] = 1.0 - 2.0 * part
    return table.reshape(2 * width, 8 * channels).astype(ml_dtypes.bfloat16)


def repeat_table(channels):
    square = channels * channels
    table = np.zeros((2, 2, channels, 2 * square + 256))
    for i in range(channels):
        for part in range(2):
            start = part * square + i * channels
            table[part, 0, i, start : start + channels] = 1.0
            table[part, 1, i, 2 * square + part * 128 + i : 2 * square + part * 128 + 128 : channels] = 1.0
    return table.reshape(4 * channels, -1).astype(ml_dtypes.bfloat16)


def forward_kernel(
    cells, field_hbm, cot_hbm, table_hbm, out_ref, data_ref, table_ref, spread_ref, rows_ref, sems
):
    channels, length_y, length_z = field_hbm.shape
    copies = []

    def start(source, target):
        copy = pltpu.make_async_copy(source, target, sems.at[len(copies)])
        copy.start()
        copies.append(copy)
        return copy

    chunks = [start(field_hbm, data_ref.at[0])]
    table = start(table_hbm, table_ref)
    chunks.append(start(cot_hbm, data_ref.at[1]))
    table.wait()
    along_y = jnp.concatenate([table_ref[:ROWS, :length_y], table_ref[:ROWS, length_y:]], axis=0)
    group = lax.broadcasted_iota(jnp.int32, (16, 256), 1) // M % 8
    for place in range(8):
        keep = jnp.where(group == place, 1.0, 0.0).astype(BF16)
        keep = jnp.concatenate([keep] * (length_z // 16), axis=0)
        for term in range(2):
            first = ROWS + term * length_z
            spread_ref[place, term * length_z : (term + 1) * length_z, :] = (
                table_ref[first : first + length_z, :] * keep
            )
    for array, copy in enumerate(chunks):
        copy.wait()
        for pair in range(channels // 2):
            data = jnp.concatenate([data_ref[array, 2 * pair], data_ref[array, 2 * pair + 1]], axis=1)
            both = dot(along_y, data)
            value = both[:PITCH] + both[ROWS : ROWS + PITCH]
            base = (array * channels + 2 * pair) * PITCH
            rows_ref[base : base + PITCH, :] = value[:, :length_z]
            rows_ref[base + PITCH : base + 2 * PITCH, :] = value[:, length_z:]
    kz = lax.broadcasted_iota(jnp.int32, (1, 128), 1) % M
    scale = jnp.where(kz == 0, 1.0 / cells, 2.0 / cells).astype(F32)
    count = 2 * channels
    lefts, rights = [], []
    for place in range(8):
        table_high, table_low = spread_ref[place, :length_z], spread_ref[place, length_z:]
        sources = [part * M + octet * 8 + place for part in range(2) for octet in range(2)]
        if place == 0:
            sources += [2 * M, 2 * M + 1]
        rows = [rows_ref[pl.ds(source, count, stride=PITCH), :] for source in sources]
        high, low = split(jnp.concatenate(rows, axis=0))
        left = jnp.concatenate([high, low, high], axis=1)
        right = jnp.concatenate([table_high, table_high, table_low], axis=0)
        if place == 0:
            last = dot(left[4 * count :], right)
            left = left[: 4 * count]
        lefts.append(left)
        rights.append(right)
    total = dot(jnp.concatenate(lefts, axis=1), jnp.concatenate(rights, axis=0))

    def turned(real, imag, sign):
        if sign > 0:
            block = (real[:, :128] + imag[:, 128:], imag[:, :128] - real[:, 128:])
        else:
            block = (real[:, :128] - imag[:, 128:], -imag[:, :128] - real[:, 128:])
        scaled = []
        for part in block:
            scaled += [part[:channels], part[channels:] * scale]
        return jnp.concatenate(scaled, axis=0).T

    for octet in range(2):
        real = total[octet * count : (octet + 1) * count]
        imag = total[(2 + octet) * count : (3 + octet) * count]
        out_ref[octet * 128 : (octet + 1) * 128, :] = turned(real, imag, 1)
        minus = turned(real, imag, -1)
        for place in range(8):
            k = octet * 8 + place
            if k > 0:
                out_ref[(2 * M - k) * M : (2 * M - k + 1) * M, :] = minus[place * M : (place + 1) * M]
    out_ref[M * M : (M + 1) * M, :] = turned(last[:count], last[count:], -1)[:M]


def mid_kernel(
    samples, planes_ref, weight_ref, fx_ref, ix_ref, spread_ref, gather_ref,
    mine_ref, other_ref, out_ref, rows_ref, split_ref,
):
    pairs, kept_x, _ = weight_ref.shape
    width_x = planes_ref.shape[0] // pairs
    pack = width_x * pairs // out_ref.shape[0]
    share = kept_x // samples
    me = lax.axis_index("dp")
    lane = lax.broadcasted_iota(jnp.int32, (width_x, 128), 1)
    sign = jnp.where(lane < 64, 1.0, -1.0).astype(F32)
    for step in range(pairs // 2):
        columns = []
        for q in (2 * step, 2 * step + 1):
            plane = planes_ref[pl.ds(q, width_x, stride=pairs), :]
            turned = pltpu.roll(plane, 64, 1) * sign
            columns.append(jnp.concatenate([plane, turned], axis=0))
        high, low = split(jnp.concatenate(columns, axis=1))
        modes = dot(fx_ref[...], jnp.concatenate([high, low, high], axis=0))
        for index, q in enumerate((2 * step, 2 * step + 1)):
            mode = modes[:, index * 128 : (index + 1) * 128]
            rows_ref[q * kept_x : (q + 1) * kept_x, :] = mode
    for q in range(pairs):
        for ahead in range(samples):
            start = q * kept_x + lax.rem(me + ahead, samples) * share
            part = rows_ref[pl.ds(pl.multiple_of(start, share), share), :]
            if ahead == 0:
                mine_ref[q] = part
            else:
                other_ref[(ahead - 1) * pairs + q] = part

    square = weight_ref.shape[2] // 2
    width = square >> LEVELS
    lane = lax.broadcasted_iota(jnp.int32, (kept_x, 128), 1)

    def merge(one, two, shift):
        first = lane & shift == 0
        moved = jnp.where(first, two, one)
        moved = jnp.take_along_axis(moved, lane ^ shift, axis=1, mode="promise_in_bounds")
        return jnp.where(first, one, two) + moved

    def products(rows, q, start):
        real, imag = rows[:, :128], rows[:, 128:]
        w_real = weight_ref[q, :, start : start + 128].astype(F32)
        w_imag = weight_ref[q, :, square + start : square + start + 128].astype(F32)
        return real * w_real + imag * w_imag, imag * w_real - real * w_imag

    grads = []
    chunk = 8
    for first in range(0, pairs, chunk):
        high, low = split(rows_ref[first * kept_x : (first + chunk) * kept_x, :])
        spread = dot(jnp.concatenate([high, low], axis=1), spread_ref[...])
        size = chunk * kept_x
        base = 2 * first * kept_x
        for place in range(chunk):
            rows = spread[place * kept_x : (place + 1) * kept_x]
            at = base + place * kept_x
            for column in range(0, width, 128):
                items = [
                    products(rows, first + place, start)
                    for start in range(column << LEVELS, column + 128 << LEVELS, 128)
                ]
                for part in range(2):
                    values = [item[part] for item in items]
                    for level in range(LEVELS):
                        values = [merge(one, two, 16 >> level) for one, two in zip(values[::2], values[1::2])]
                    high, low = split(values[0])
                    at_column = part * width + column
                    split_ref[at : at + kept_x, at_column : at_column + 128] = high
                    split_ref[at + size : at + size + kept_x, at_column : at_column + 128] = low
        both = dot(split_ref[base : base + 2 * size, :], gather_ref[...])
        grads.append(both[:size] + both[size:])
    grads = jnp.concatenate(grads, axis=0)
    count = pairs // pack
    if pack == 2:
        size = count * kept_x
        lane = lax.broadcasted_iota(jnp.int32, (size, 256), 1) % 128
        grads = jnp.where(lane < 64, grads[:size], grads[size:])
    for step in range(count // 2):
        columns = []
        for row in (2 * step, 2 * step + 1):
            block = grads[row * kept_x : (row + 1) * kept_x]
            columns.append(jnp.concatenate([block[:, :128], block[:, 128:]], axis=0))
        high, low = split(jnp.concatenate(columns, axis=1))
        planes = dot(ix_ref[...], jnp.concatenate([high, low, high], axis=0))
        for index, row in enumerate((2 * step, 2 * step + 1)):
            out_ref[pl.ds(row, width_x, stride=count), :] = planes[:, index * 128 : (index + 1) * 128]


def weight_terms_in(modes_ref, repeat_ref, part, emit):
    square = (repeat_ref.shape[1] - 256) // 2
    rows = modes_ref[part]
    shape = rows.shape[:2] + (256,)
    high, low = split(rows.reshape(shape[0] * shape[1], 128))
    side = jnp.concatenate([high, low], axis=1)

    def repeated(start):
        table = repeat_ref[:, start : start + 256]
        return dot(side, jnp.concatenate([table, table], axis=0))

    cots = repeated(2 * square)
    c_real = jnp.concatenate([cots[:, :128]] * 2, axis=1)
    c_imag = jnp.concatenate([cots[:, 128:]] * 2, axis=1)
    for start in range(0, square, 256):
        f_real, f_imag = repeated(start), repeated(square + start)
        emit(start, (f_real * c_real + f_imag * c_imag).reshape(shape))
        emit(square + start, (f_real * c_imag - f_imag * c_real).reshape(shape))


def weight_kernel(modes_ref, repeat_ref, before_ref, out_hbm, out_ref, sems):
    pairs = modes_ref.shape[0]
    copies = []
    for first in range(0, pairs, pairs // 4):
        part = pl.ds(first, pairs // 4)

        def emit(start, value):
            out_ref[part, :, start : start + 256] = before_ref[part, :, start : start + 256] + value

        weight_terms_in(modes_ref, repeat_ref, part, emit)
        copies.append(pltpu.make_async_copy(out_ref.at[part], out_hbm.at[part], sems.at[len(copies)]))
        copies[-1].start()
    for copy in copies:
        copy.wait()


def local_kernel(kept, *refs):
    cot_hbm, weight_ref = refs[:2]
    linear_ref, cot_ref, mix_ref, sem = refs[kept + 2], *refs[-3:]
    copy = pltpu.make_async_copy(cot_hbm, cot_ref, sem)
    copy.start()
    if kept:
        modes_ref, repeat_ref, out_ref = refs[2], refs[3], refs[5]
        pairs = modes_ref.shape[0]
        for first in range(0, pairs, pairs // 4):
            part = pl.ds(first, pairs // 4)

            def emit(start, value):
                out_ref[part, :, start : start + 256] = value

            weight_terms_in(modes_ref, repeat_ref, part, emit)
    channels, length_y, length_z = cot_ref.shape
    size = 16 * channels
    left = lax.broadcasted_iota(jnp.int32, (size, channels), 0) // 16 == lax.broadcasted_iota(
        jnp.int32, (size, channels), 1
    )
    right = lax.broadcasted_iota(jnp.int32, (channels, size), 1) // 16 == lax.broadcasted_iota(
        jnp.int32, (channels, size), 0
    )
    tall = dot(left.astype(F32).astype(BF16), weight_ref[...]).astype(BF16)
    wide = dot(tall, right.astype(F32).astype(BF16))
    same = lax.broadcasted_iota(jnp.int32, (size, size), 0) % 16 == lax.broadcasted_iota(
        jnp.int32, (size, size), 1
    ) % 16
    mix_ref[...] = jnp.where(same, wide, 0.0).astype(BF16)
    copy.wait()
    for step in range(length_y // 32):
        columns = []
        for part in range(2):
            first = step * 32 + part * 16
            columns.append(cot_ref[:, first : first + 16, :].reshape(channels * 16, length_z))
        mixed = dot(mix_ref[...], jnp.concatenate(columns, axis=1))
        for part in range(2):
            first = step * 32 + part * 16
            linear_ref[:, first : first + 16, :] = mixed[:, part * length_z : (part + 1) * length_z].reshape(
                channels, 16, length_z
            )


def inverse_kernel(planes_ref, linear_ref, iz_ref, iy_ref, out_hbm, rows_ref, out_ref, sems):
    channels, _, length_z = linear_ref.shape
    rows = planes_ref.shape[0]
    pitch = channels + 8
    pack = 2 * M * M // rows
    group = lax.broadcasted_iota(jnp.int32, (16, 256), 1) // M % 8
    keeps = []
    for step in range(4):
        keep = jnp.where(group // 2 == step, 1.0, 0.0).astype(BF16)
        keeps.append(jnp.concatenate([keep] * (channels // 16), axis=0))
    lane = lax.broadcasted_iota(jnp.int32, (M, 128), 1)

    def block(index):
        return planes_ref[index * M : (index + 1) * M, :]

    def halves(turned):
        found = []
        for low_bit in range(pack):
            first = low_bit * 2 * channels
            found.append(
                jnp.concatenate(
                    [turned[first : first + channels], turned[first + channels : first + 2 * channels]], axis=1
                )
            )
        return found

    def along_z(parts, which, steps):
        terms = [split(part) for part in parts]
        left = []
        for step in steps:
            for high, low in terms:
                high, low = high * keeps[step], low * keeps[step]
                left.append(jnp.concatenate([high, low, high], axis=1))
        right = jnp.concatenate([iz_ref[which, 0], iz_ref[which, 0], iz_ref[which, 1]], axis=0)
        return dot(jnp.concatenate(left, axis=0), right)

    def put(value, part, k):
        first = mode_row(part, k) * pitch
        rows_ref[first : first + channels, :] = value

    blocks = rows // M
    octets = blocks // 16
    for octet in range(octets):
        sums, differences = [], []
        for place in range(8):
            index = octet * 8 + place
            plus = block(index)
            minus = block(blocks - index) if index > 0 else jnp.zeros_like(plus)
            if pack == 2:
                minus = jnp.where(lane < 64, minus, block(blocks - 1 - index))
            sums.append(plus + minus)
            differences.append(plus - minus)
        for part, stack in enumerate((sums, differences)):
            parts = halves(jnp.concatenate(stack, axis=0).T)
            value = along_z(parts, part, range(4))
            for step in range(4):
                for low_bit in range(pack):
                    first = (step * pack + low_bit) * channels
                    for parity in range(2):
                        k = (octet * 8 + step * 2 + parity) * pack + low_bit
                        put(
                            value[first : first + channels, parity * length_z : (parity + 1) * length_z],
                            part,
                            k,
                        )
    last = block(blocks // 2)
    last = jnp.concatenate([last, jnp.zeros((128 - M, 128), F32)], axis=0).T
    first_half = halves(last)[:1]
    put(along_z(first_half, 0, [0])[:, :length_z], 0, M)
    put(-along_z(first_half, 1, [0])[:, :length_z], 1, M)
    rows_ref[(2 * M + 2) * pitch :, :] = jnp.zeros(((ROWS - 2 * M - 2) * pitch, length_z), F32)
    copies = []
    for pair in range(channels // 2):
        columns = [rows_ref[pl.ds(2 * pair + side, ROWS, stride=pitch), :] for side in range(2)]
        high, low = split(jnp.concatenate(columns, axis=1))
        value = dot(iy_ref[...], jnp.concatenate([high, low, high], axis=0))
        for side in range(2):
            channel = 2 * pair + side
            spectral = value[:, side * length_z : (side + 1) * length_z]
            out_ref[channel] = (spectral + linear_ref[channel]).astype(BF16)
        if pair % 4 == 3:
            part = pl.ds(2 * pair - 6, 8)
            copies.append(pltpu.make_async_copy(out_ref.at[part], out_hbm.at[part], sems.at[len(copies)]))
            copies[-1].start()
    for copy in copies:
        copy.wait()


def in_hbm(value):
    return pltpu.with_memory_space_constraint(value, pltpu.HBM)


def call(kernel, out_shape, scratch, limit, flops, moved, *args, **kwargs):
    return pl.pallas_call(
        kernel,
        out_shape=out_shape,
        **kwargs,
        scratch_shapes=scratch,
        compiler_params=pltpu.CompilerParams(vmem_limit_bytes=limit * MIB),
        cost_estimate=pl.CostEstimate(flops=flops, bytes_accessed=moved, transcendentals=0),
    )(*args)


def weight_terms(modes, channels):
    parts = modes.reshape(modes.shape[:3] + (2, 2, channels))
    in_real, in_imag = parts[..., 0, 0, :, None], parts[..., 1, 0, :, None]
    cot_real, cot_imag = parts[..., 0, 1, None, :], parts[..., 1, 1, None, :]
    real = jnp.sum(in_real * cot_real + in_imag * cot_imag, axis=0)
    imag = jnp.sum(in_real * cot_imag - in_imag * cot_real, axis=0)
    stacked = jnp.stack([real, imag], axis=2)
    return stacked.reshape(stacked.shape[:2] + (-1,))


def on_device(field, cotangent, spectral_weight, pointwise_weight):
    _, planes, channels, length_y, length_z = field.shape
    pairs, kept_x, _ = spectral_weight.shape
    groups = lax.axis_size("gx")
    samples = lax.axis_size("dp")
    width_x = planes * groups
    share = kept_x // samples
    pack = 2 if pairs == 2 * M else 1
    count = pairs // pack
    all_pairs = 2 * M * M
    cells = width_x * length_y * length_z
    shape = jax.ShapeDtypeStruct
    field = field.reshape(channels, length_y, length_z)
    cotangent = cotangent.reshape(channels, length_y, length_z)

    forward = forward_tables(length_y, length_z)
    iz, iy = inverse_tables(length_y, length_z)
    fx, ix = x_tables(kept_x, width_x)
    hbm = pl.BlockSpec(memory_space=pltpu.HBM)
    spectra = call(
        functools.partial(forward_kernel, cells),
        pltpu.VMEM((all_pairs, 128), F32),
        [
            pltpu.VMEM((2,) + field.shape, BF16),
            pltpu.VMEM(forward.shape, BF16),
            pltpu.VMEM((8, 2 * length_z, 256), BF16),
            pltpu.VMEM((2 * channels * PITCH, length_z), F32),
            pltpu.SemaphoreType.DMA((3,)),
        ],
        16, 10**9, 5 * 10**6,
        *[in_hbm(one) for one in (field, cotangent, forward)],
        in_specs=[hbm] * 3,
    )
    spectra, spectral_weight, spread, gather = lax.optimization_barrier(
        (spectra, spectral_weight, spread_table(channels), gather_table(channels))
    )
    received = lax.all_to_all(
        spectra.reshape(groups, pairs, 128), "gx", split_axis=0, concat_axis=0, tiled=True
    )
    mine, other, grads = call(
        functools.partial(mid_kernel, samples),
        (
            pltpu.VMEM((pairs, share, 128), F32),
            pltpu.VMEM((pairs * (samples - 1), share, 128), F32),
            pltpu.VMEM((width_x * count, 128), F32),
        ),
        [
            pltpu.VMEM((pairs * kept_x, 128), F32),
            pltpu.VMEM((2 * pairs * kept_x, gather.shape[0]), BF16),
        ],
        16, 10**9, 4 * 10**6,
        received.reshape(width_x * pairs, 128), spectral_weight, fx, ix, spread, gather,
    )
    returned = lax.all_to_all(
        grads.reshape(groups, count, 128), "gx", split_axis=0, concat_axis=0, tiled=True
    )
    split_samples = samples == 2 and share % 8 == 0
    kept = [mine, repeat_table(channels)] if split_samples else []
    tall = (pairs, share, 2 * channels * channels)
    _, late = lax.optimization_barrier((grads, cotangent))
    linear, *weight_grad = call(
        functools.partial(local_kernel, len(kept)),
        [shape((channels, length_y, length_z), F32)] + [shape(tall, F32)] * (len(kept) // 2),
        [
            pltpu.VMEM((channels, length_y, length_z), BF16),
            pltpu.VMEM((16 * channels, 16 * channels), BF16),
            pltpu.SemaphoreType.DMA(()),
        ],
        16, 4 * 10**9, 5 * 10**6,
        in_hbm(late), pointwise_weight, *kept,
        in_specs=[hbm] + [pl.BlockSpec()] * (1 + len(kept)),
    )
    if split_samples:
        other = lax.ppermute(other, "dp", [(0, 1), (1, 0)])
        weight_grad = call(
            weight_kernel,
            shape(tall, F32),
            [pltpu.VMEM(tall, F32), pltpu.SemaphoreType.DMA((4,))],
            16, 2 * 10**9, 5 * 10**6,
            other, kept[1], *weight_grad,
            out_specs=hbm,
        )
    else:
        me = lax.axis_index("dp")
        modes = jnp.concatenate([mine[None], other.reshape(samples - 1, pairs, share, 128)])
        modes = jnp.roll(modes, me, 0)
        modes = lax.all_to_all(modes, "dp", split_axis=0, concat_axis=0, tiled=True)
        weight_grad = weight_terms(modes, channels)
    field_grad = call(
        inverse_kernel,
        shape((channels, length_y, length_z), BF16),
        [
            pltpu.VMEM((ROWS * (channels + 8), length_z), F32),
            pltpu.VMEM((channels, length_y, length_z), BF16),
            pltpu.SemaphoreType.DMA((channels // 8,)),
        ],
        16, 10**9, 4 * 10**6,
        returned.reshape(width_x * count, 128), linear, iz, iy,
        out_specs=hbm,
    )
    return field_grad.reshape(1, planes, channels, length_y, length_z), weight_grad


def solution(mesh):
    placed = (
        P("dp", "gx", None, None, None),
        P("dp", "gx", None, None, None),
        P("gx", None, None),
        P(),
    )
    return jax.shard_map(
        on_device,
        mesh=mesh,
        in_specs=placed,
        out_specs=(P("dp", "gx", None, None, None), P("gx", "dp", None)),
        check_vma=False,
    )
```

```python
import functools
import math

import jax
import jax.numpy as jnp
import ml_dtypes
import numpy as np
from jax import lax
from jax.experimental import pallas as pl
from jax.experimental.pallas import tpu as pltpu
from jax.sharding import PartitionSpec as P

M = 16
F32 = jnp.float32
BF16 = jnp.bfloat16
MIB = 1024 * 1024
ROWS = 3 * M
PITCH = ROWS - 8


def kept_freqs(half_count, length):
    index = np.arange(2 * half_count)
    return np.where(index < half_count, index, index + length - 2 * half_count)


def phases(frequency, length):
    product = np.outer(frequency, np.arange(length)) % length
    angle = product * (2.0 * math.pi / length)
    return np.cos(angle), np.sin(angle)


def split_np(table):
    high = table.astype(ml_dtypes.bfloat16)
    low = (table - high.astype(np.float64)).astype(ml_dtypes.bfloat16)
    return high, low


def split(value):
    high = value.astype(BF16)
    low = (value - high.astype(F32)).astype(BF16)
    return high, low


def dot(left, right):
    return jnp.dot(left, right, preferred_element_type=F32)


def forward_tables(length_y, length_z):
    cos_y, sin_y = phases(np.arange(M + 1), length_y)
    rows = np.zeros((ROWS, length_y))
    rows[:M], rows[M : 2 * M] = cos_y[:M], -sin_y[:M]
    rows[2 * M], rows[2 * M + 1] = cos_y[M], -sin_y[M]
    along_y = np.concatenate(split_np(rows), 1)
    cos_z, sin_z = phases(np.arange(M), length_z)
    along_z = np.concatenate([np.tile(cos_z.T, (1, 8)), np.tile(sin_z.T, (1, 8))], 1)
    return np.concatenate((along_y,) + split_np(along_z))


def inverse_tables(length_y, length_z):
    cos_z, sin_z = phases(np.arange(M), length_z)
    along_z = np.zeros((2, 2, 8, M, 2, length_z))
    for place in range(8):
        along_z[0, 0, place, :, place % 2] = cos_z
        along_z[0, 1, place, :, place % 2] = -sin_z
        along_z[1, 0, place, :, place % 2] = sin_z
        along_z[1, 1, place, :, place % 2] = cos_z
    along_z = along_z.reshape(2, 2 * 8 * M, 2 * length_z)
    along_z = np.stack([np.stack(split_np(part)) for part in along_z])
    cos_y, sin_y = phases(np.arange(M + 1), length_y)
    columns = np.zeros((length_y, ROWS))
    for k in range(M + 1):
        columns[:, mode_row(0, k)] = cos_y[k]
        columns[:, mode_row(1, k)] = -sin_y[k]
    high, low = split_np(columns)
    return along_z, np.concatenate([high, high, low], 1)


def mode_row(part, k):
    return 2 * M + part if k == M else part * M + k


def x_tables(kept_x, width_x):
    cos_x, sin_x = phases(kept_freqs(kept_x // 2, width_x), width_x)
    high, low = split_np(np.concatenate([cos_x, sin_x], 1))
    forward = np.concatenate([high, high, low], 1)
    high, low = split_np(np.concatenate([cos_x.T, sin_x.T], 1))
    inverse = np.concatenate([high, high, low], 1)
    return forward, inverse


def spread_table(channels):
    copies = 128 // channels
    table = np.zeros((2, 2, 2, channels, 2, 2, copies, channels))
    eye = np.eye(channels)
    for part in range(2):
        table[:, part, 1, :, 0, part] = eye[:, None, :]
        table[:, part, 1, :, 1, part] = eye[:, None, np.arange(channels) ^ 16]
    return table.reshape(8 * channels, 512).astype(ml_dtypes.bfloat16)


def pair_table():
    lane = np.arange(128)
    first = (lane & 16) * 8
    table = np.zeros((256, 256))
    table[first + lane, lane] = 1.0
    table[first + (lane ^ 16), 128 + lane] = 1.0
    return table.astype(ml_dtypes.bfloat16)


def gather_table(channels):
    width = channels * channels // 2
    place = np.arange(width)
    lane = place % 128
    i = (place // 128 * 2 + (lane & 16) // 16) * (128 // channels) + lane // channels
    table = np.zeros((2, width, 2, 2, 2, channels))
    for part in range(2):
        table[part, place, 0, :, part, i] = 1.0
        table[part, place, 1, :, 1 - part, i] = 1.0 - 2.0 * part
    return table.reshape(2 * width, 8 * channels).astype(ml_dtypes.bfloat16)


def repeat_table(channels):
    square = channels * channels
    table = np.zeros((2, 2, channels, 2 * square + 256))
    for i in range(channels):
        for part in range(2):
            start = part * square + i * channels
            table[part, 0, i, start : start + channels] = 1.0
            table[part, 1, i, 2 * square + part * 128 + i : 2 * square + part * 128 + 128 : channels] = 1.0
    return table.reshape(4 * channels, -1).astype(ml_dtypes.bfloat16)


def forward_kernel(
    cells, field_hbm, cot_hbm, table_hbm, out_ref, data_ref, table_ref, spread_ref, rows_ref, sems
):
    channels, length_y, length_z = field_hbm.shape
    copies = []

    def start(source, target):
        copy = pltpu.make_async_copy(source, target, sems.at[len(copies)])
        copy.start()
        copies.append(copy)
        return copy

    table = start(table_hbm, table_ref)
    chunks = [start(ref, data_ref.at[array]) for array, ref in enumerate((field_hbm, cot_hbm))]
    table.wait()
    along_y = jnp.concatenate([table_ref[:ROWS, :length_y], table_ref[:ROWS, length_y:]], axis=0)
    group = lax.broadcasted_iota(jnp.int32, (16, 256), 1) // M % 8
    for place in range(8):
        keep = jnp.where(group == place, 1.0, 0.0).astype(BF16)
        keep = jnp.concatenate([keep] * (length_z // 16), axis=0)
        for term in range(2):
            first = ROWS + term * length_z
            spread_ref[place, term * length_z : (term + 1) * length_z, :] = (
                table_ref[first : first + length_z, :] * keep
            )
    for array, copy in enumerate(chunks):
        copy.wait()
        for pair in range(channels // 2):
            data = jnp.concatenate([data_ref[array, 2 * pair], data_ref[array, 2 * pair + 1]], axis=1)
            both = dot(along_y, data)
            value = both[:PITCH] + both[ROWS : ROWS + PITCH]
            base = (array * channels + 2 * pair) * PITCH
            rows_ref[base : base + PITCH, :] = value[:, :length_z]
            rows_ref[base + PITCH : base + 2 * PITCH, :] = value[:, length_z:]
    kz = lax.broadcasted_iota(jnp.int32, (1, 128), 1) % M
    scale = jnp.where(kz == 0, 1.0 / cells, 2.0 / cells).astype(F32)
    count = 2 * channels
    lefts, rights = [], []
    for place in range(8):
        table_high, table_low = spread_ref[place, :length_z], spread_ref[place, length_z:]
        sources = [part * M + octet * 8 + place for part in range(2) for octet in range(2)]
        if place == 0:
            sources += [2 * M, 2 * M + 1]
        rows = [rows_ref[pl.ds(source, count, stride=PITCH), :] for source in sources]
        high, low = split(jnp.concatenate(rows, axis=0))
        left = jnp.concatenate([high, low, high], axis=1)
        right = jnp.concatenate([table_high, table_high, table_low], axis=0)
        if place == 0:
            last = dot(left[4 * count :], right)
            left = left[: 4 * count]
        lefts.append(left)
        rights.append(right)
    total = dot(jnp.concatenate(lefts, axis=1), jnp.concatenate(rights, axis=0))

    def turned(real, imag, sign):
        if sign > 0:
            block = (real[:, :128] + imag[:, 128:], imag[:, :128] - real[:, 128:])
        else:
            block = (real[:, :128] - imag[:, 128:], -imag[:, :128] - real[:, 128:])
        scaled = []
        for part in block:
            scaled += [part[:channels], part[channels:] * scale]
        return jnp.concatenate(scaled, axis=0).T

    for octet in range(2):
        real = total[octet * count : (octet + 1) * count]
        imag = total[(2 + octet) * count : (3 + octet) * count]
        out_ref[octet * 128 : (octet + 1) * 128, :] = turned(real, imag, 1)
        minus = turned(real, imag, -1)
        for place in range(8):
            k = octet * 8 + place
            if k > 0:
                out_ref[(2 * M - k) * M : (2 * M - k + 1) * M, :] = minus[place * M : (place + 1) * M]
    out_ref[M * M : (M + 1) * M, :] = turned(last[:count], last[count:], -1)[:M]


def mid_kernel(
    samples, planes_ref, weight_ref, fx_ref, ix_ref, spread_ref, pair_ref, gather_ref,
    mine_ref, other_ref, out_ref, rows_ref, split_ref,
):
    pairs, kept_x, _ = weight_ref.shape
    width_x = planes_ref.shape[0] // pairs
    pack = width_x * pairs // out_ref.shape[0]
    share = kept_x // samples
    me = lax.axis_index("dp")
    lane = lax.broadcasted_iota(jnp.int32, (width_x, 128), 1)
    sign = jnp.where(lane < 64, 1.0, -1.0).astype(F32)
    for step in range(pairs // 2):
        columns = []
        for q in (2 * step, 2 * step + 1):
            plane = planes_ref[pl.ds(q, width_x, stride=pairs), :]
            turned = pltpu.roll(plane, 64, 1) * sign
            columns.append(jnp.concatenate([plane, turned], axis=0))
        high, low = split(jnp.concatenate(columns, axis=1))
        modes = dot(fx_ref[...], jnp.concatenate([high, low, high], axis=0))
        for index, q in enumerate((2 * step, 2 * step + 1)):
            mode = modes[:, index * 128 : (index + 1) * 128]
            rows_ref[q * kept_x : (q + 1) * kept_x, :] = mode
    for q in range(pairs):
        for ahead in range(samples):
            start = q * kept_x + lax.rem(me + ahead, samples) * share
            part = rows_ref[pl.ds(pl.multiple_of(start, share), share), :]
            if ahead == 0:
                mine_ref[q] = part
            else:
                other_ref[(ahead - 1) * pairs + q] = part

    square = weight_ref.shape[2] // 2
    width = square // 2
    grads = []
    chunk = min(pairs, 8)
    for first in range(0, pairs, chunk):
        size = chunk * kept_x
        base = 2 * first * kept_x
        high, low = split(rows_ref[first * kept_x : (first + chunk) * kept_x, :])
        spread = dot(jnp.concatenate([high, low], axis=1), spread_ref[...])
        real, imag, real_s, imag_s = (spread[:, 128 * k : 128 * k + 128] for k in range(4))

        def paired(start):
            block = weight_ref[first : first + chunk, :, start : start + 256].reshape(size, 256)
            both = dot(block, pair_ref[...])
            return both[:, :128], both[:, 128:]

        lane = lax.broadcasted_iota(jnp.int32, (kept_x, 128), 1)
        lower = lane & 16 == 0

        def store(sums, at, column):
            for part in range(2):
                high, low = split(sums[part])
                at_column = part * width + column
                split_ref[base + at : base + at + kept_x, at_column : at_column + 128] = high
                split_ref[base + size + at : base + size + at + kept_x, at_column : at_column + 128] = low

        for column in range(0, width, 128):
            by_dot = column // 128 % 4 == 3
            if by_dot:
                w_real, w_real_s = paired(2 * column)
                w_imag, w_imag_s = paired(square + 2 * column)
            for place in range(chunk):
                rows = slice(place * kept_x, (place + 1) * kept_x)
                r, i, rs, im_s = real[rows], imag[rows], real_s[rows], imag_s[rows]
                if by_dot:
                    wr, wi, wrs, wis = w_real[rows], w_imag[rows], w_real_s[rows], w_imag_s[rows]
                    sums = (
                        (r * wr + i * wi) + (rs * wrs + im_s * wis),
                        (i * wr - r * wi) + (im_s * wrs - rs * wis),
                    )
                else:
                    found = []
                    for start in (2 * column, 2 * column + 128):
                        wr = weight_ref[first + place, :, start : start + 128].astype(F32)
                        wi = weight_ref[first + place, :, square + start : square + start + 128].astype(F32)
                        found.append((r * wr + i * wi, i * wr - r * wi))
                    sums = []
                    for one, two in zip(*found):
                        moved = jnp.where(lower, two, one)
                        moved = jnp.take_along_axis(moved, lane ^ 16, axis=1, mode="promise_in_bounds")
                        sums.append(jnp.where(lower, one, two) + moved)
                store(sums, place * kept_x, column)
        both = dot(split_ref[base : base + 2 * size, :], gather_ref[...])
        grads.append(both[:size] + both[size:])
    grads = jnp.concatenate(grads, axis=0)
    count = pairs // pack
    if pack == 2:
        size = count * kept_x
        lane = lax.broadcasted_iota(jnp.int32, (size, 256), 1) % 128
        grads = jnp.where(lane < 64, grads[:size], grads[size:])
    for step in range(count // 2):
        columns = []
        for row in (2 * step, 2 * step + 1):
            block = grads[row * kept_x : (row + 1) * kept_x]
            columns.append(jnp.concatenate([block[:, :128], block[:, 128:]], axis=0))
        high, low = split(jnp.concatenate(columns, axis=1))
        planes = dot(ix_ref[...], jnp.concatenate([high, low, high], axis=0))
        for index, row in enumerate((2 * step, 2 * step + 1)):
            out_ref[pl.ds(row, width_x, stride=count), :] = planes[:, index * 128 : (index + 1) * 128]


def weight_terms_in(modes_ref, repeat_ref, part, emit):
    square = (repeat_ref.shape[1] - 256) // 2
    rows = modes_ref[part]
    shape = rows.shape[:2] + (256,)
    high, low = split(rows.reshape(shape[0] * shape[1], 128))
    side = jnp.concatenate([high, low], axis=1)

    def repeated(start):
        table = repeat_ref[:, start : start + 256]
        return dot(side, jnp.concatenate([table, table], axis=0))

    cots = repeated(2 * square)
    c_real = jnp.concatenate([cots[:, :128]] * 2, axis=1)
    c_imag = jnp.concatenate([cots[:, 128:]] * 2, axis=1)
    for start in range(0, square, 256):
        f_real, f_imag = repeated(start), repeated(square + start)
        emit(start, (f_real * c_real + f_imag * c_imag).reshape(shape))
        emit(square + start, (f_real * c_imag - f_imag * c_real).reshape(shape))


def weight_kernel(modes_ref, repeat_ref, before_ref, out_hbm, out_ref, sems):
    pairs = modes_ref.shape[0]
    copies = []
    for first in range(0, pairs, pairs // 4):
        part = pl.ds(first, pairs // 4)

        def emit(start, value):
            out_ref[part, :, start : start + 256] = before_ref[part, :, start : start + 256] + value

        weight_terms_in(modes_ref, repeat_ref, part, emit)
        copies.append(pltpu.make_async_copy(out_ref.at[part], out_hbm.at[part], sems.at[len(copies)]))
        copies[-1].start()
    for copy in copies:
        copy.wait()


def local_kernel(kept, *refs):
    cot_hbm, weight_ref = refs[:2]
    linear_ref, cot_ref, mix_ref, sem = refs[kept + 2], *refs[-3:]
    copy = pltpu.make_async_copy(cot_hbm, cot_ref, sem)
    copy.start()
    if kept:
        modes_ref, repeat_ref, out_ref = refs[2], refs[3], refs[5]
        pairs = modes_ref.shape[0]
        for first in range(0, pairs, pairs // 4):
            part = pl.ds(first, pairs // 4)

            def emit(start, value):
                out_ref[part, :, start : start + 256] = value

            weight_terms_in(modes_ref, repeat_ref, part, emit)
    channels, length_y, length_z = cot_ref.shape
    size = 16 * channels
    left = lax.broadcasted_iota(jnp.int32, (size, channels), 0) // 16 == lax.broadcasted_iota(
        jnp.int32, (size, channels), 1
    )
    right = lax.broadcasted_iota(jnp.int32, (channels, size), 1) // 16 == lax.broadcasted_iota(
        jnp.int32, (channels, size), 0
    )
    tall = dot(left.astype(F32).astype(BF16), weight_ref[...]).astype(BF16)
    wide = dot(tall, right.astype(F32).astype(BF16))
    same = lax.broadcasted_iota(jnp.int32, (size, size), 0) % 16 == lax.broadcasted_iota(
        jnp.int32, (size, size), 1
    ) % 16
    mix_ref[...] = jnp.where(same, wide, 0.0).astype(BF16)
    copy.wait()
    for step in range(length_y // 32):
        columns = []
        for part in range(2):
            first = step * 32 + part * 16
            columns.append(cot_ref[:, first : first + 16, :].reshape(channels * 16, length_z))
        mixed = dot(mix_ref[...], jnp.concatenate(columns, axis=1))
        for part in range(2):
            first = step * 32 + part * 16
            linear_ref[:, first : first + 16, :] = mixed[:, part * length_z : (part + 1) * length_z].reshape(
                channels, 16, length_z
            )


def inverse_kernel(planes_ref, linear_ref, iz_ref, iy_ref, out_hbm, rows_ref, out_ref, sems):
    channels, _, length_z = linear_ref.shape
    rows = planes_ref.shape[0]
    pitch = channels + 8
    pack = 2 * M * M // rows
    group = lax.broadcasted_iota(jnp.int32, (16, 256), 1) // M % 8
    keeps = []
    for step in range(4):
        keep = jnp.where(group // 2 == step, 1.0, 0.0).astype(BF16)
        keeps.append(jnp.concatenate([keep] * (channels // 16), axis=0))
    lane = lax.broadcasted_iota(jnp.int32, (M, 128), 1)

    def block(index):
        return planes_ref[index * M : (index + 1) * M, :]

    def halves(turned):
        found = []
        for low_bit in range(pack):
            first = low_bit * 2 * channels
            found.append(
                jnp.concatenate(
                    [turned[first : first + channels], turned[first + channels : first + 2 * channels]], axis=1
                )
            )
        return found

    def along_z(parts, which, steps):
        terms = [split(part) for part in parts]
        left = []
        for step in steps:
            for high, low in terms:
                high, low = high * keeps[step], low * keeps[step]
                left.append(jnp.concatenate([high, low, high], axis=1))
        right = jnp.concatenate([iz_ref[which, 0], iz_ref[which, 0], iz_ref[which, 1]], axis=0)
        return dot(jnp.concatenate(left, axis=0), right)

    def put(value, part, k):
        first = mode_row(part, k) * pitch
        rows_ref[first : first + channels, :] = value

    blocks = rows // M
    octets = blocks // 16
    for octet in range(octets):
        sums, differences = [], []
        for place in range(8):
            index = octet * 8 + place
            plus = block(index)
            minus = block(blocks - index) if index > 0 else jnp.zeros_like(plus)
            if pack == 2:
                minus = jnp.where(lane < 64, minus, block(blocks - 1 - index))
            sums.append(plus + minus)
            differences.append(plus - minus)
        for part, stack in enumerate((sums, differences)):
            parts = halves(jnp.concatenate(stack, axis=0).T)
            value = along_z(parts, part, range(4))
            for step in range(4):
                for low_bit in range(pack):
                    first = (step * pack + low_bit) * channels
                    for parity in range(2):
                        k = (octet * 8 + step * 2 + parity) * pack + low_bit
                        put(
                            value[first : first + channels, parity * length_z : (parity + 1) * length_z],
                            part,
                            k,
                        )
    last = block(blocks // 2)
    last = jnp.concatenate([last, jnp.zeros((128 - M, 128), F32)], axis=0).T
    first_half = halves(last)[:1]
    put(along_z(first_half, 0, [0])[:, :length_z], 0, M)
    put(-along_z(first_half, 1, [0])[:, :length_z], 1, M)
    rows_ref[(2 * M + 2) * pitch :, :] = jnp.zeros(((ROWS - 2 * M - 2) * pitch, length_z), F32)
    copies = []
    for pair in range(channels // 2):
        columns = [rows_ref[pl.ds(2 * pair + side, ROWS, stride=pitch), :] for side in range(2)]
        high, low = split(jnp.concatenate(columns, axis=1))
        value = dot(iy_ref[...], jnp.concatenate([high, low, high], axis=0))
        for side in range(2):
            channel = 2 * pair + side
            spectral = value[:, side * length_z : (side + 1) * length_z]
            out_ref[channel] = (spectral + linear_ref[channel]).astype(BF16)
        if pair % 4 == 3:
            part = pl.ds(2 * pair - 6, 8)
            copies.append(pltpu.make_async_copy(out_ref.at[part], out_hbm.at[part], sems.at[len(copies)]))
            copies[-1].start()
    for copy in copies:
        copy.wait()


def in_hbm(value):
    return pltpu.with_memory_space_constraint(value, pltpu.HBM)


def call(kernel, out_shape, scratch, limit, flops, moved, *args, **kwargs):
    return pl.pallas_call(
        kernel,
        out_shape=out_shape,
        **kwargs,
        scratch_shapes=scratch,
        compiler_params=pltpu.CompilerParams(vmem_limit_bytes=limit * MIB),
        cost_estimate=pl.CostEstimate(flops=flops, bytes_accessed=moved, transcendentals=0),
    )(*args)


def weight_terms(modes, channels):
    parts = modes.reshape(modes.shape[:3] + (2, 2, channels))
    in_real, in_imag = parts[..., 0, 0, :, None], parts[..., 1, 0, :, None]
    cot_real, cot_imag = parts[..., 0, 1, None, :], parts[..., 1, 1, None, :]
    real = jnp.sum(in_real * cot_real + in_imag * cot_imag, axis=0)
    imag = jnp.sum(in_real * cot_imag - in_imag * cot_real, axis=0)
    stacked = jnp.stack([real, imag], axis=2)
    return stacked.reshape(stacked.shape[:2] + (-1,))


def on_device(field, cotangent, spectral_weight, pointwise_weight):
    _, planes, channels, length_y, length_z = field.shape
    pairs, kept_x, _ = spectral_weight.shape
    groups = lax.axis_size("gx")
    samples = lax.axis_size("dp")
    width_x = planes * groups
    share = kept_x // samples
    pack = 2 if pairs == 2 * M else 1
    count = pairs // pack
    all_pairs = 2 * M * M
    cells = width_x * length_y * length_z
    shape = jax.ShapeDtypeStruct
    field = field.reshape(channels, length_y, length_z)
    cotangent = cotangent.reshape(channels, length_y, length_z)

    forward = forward_tables(length_y, length_z)
    iz, iy = inverse_tables(length_y, length_z)
    fx, ix = x_tables(kept_x, width_x)
    hbm = pl.BlockSpec(memory_space=pltpu.HBM)
    spectra = call(
        functools.partial(forward_kernel, cells),
        pltpu.VMEM((all_pairs, 128), F32),
        [
            pltpu.VMEM((2,) + field.shape, BF16),
            pltpu.VMEM(forward.shape, BF16),
            pltpu.VMEM((8, 2 * length_z, 256), BF16),
            pltpu.VMEM((2 * channels * PITCH, length_z), F32),
            pltpu.SemaphoreType.DMA((3,)),
        ],
        16, 10**9, 5 * 10**6,
        *[in_hbm(one) for one in (field, cotangent, forward)],
        in_specs=[hbm] * 3,
    )
    spectra, spectral_weight, spread, gather = lax.optimization_barrier(
        (spectra, spectral_weight, spread_table(channels), gather_table(channels))
    )
    received = lax.all_to_all(
        spectra.reshape(groups, pairs, 128), "gx", split_axis=0, concat_axis=0, tiled=True
    )
    mine, other, grads = call(
        functools.partial(mid_kernel, samples),
        (
            pltpu.VMEM((pairs, share, 128), F32),
            pltpu.VMEM((pairs * (samples - 1), share, 128), F32),
            pltpu.VMEM((width_x * count, 128), F32),
        ),
        [
            pltpu.VMEM((pairs * kept_x, 128), F32),
            pltpu.VMEM((2 * pairs * kept_x, gather.shape[0]), BF16),
        ],
        16, 10**9, 4 * 10**6,
        received.reshape(width_x * pairs, 128), spectral_weight, fx, ix, spread, pair_table(), gather,
    )
    returned = lax.all_to_all(
        grads.reshape(groups, count, 128), "gx", split_axis=0, concat_axis=0, tiled=True
    )
    split_samples = samples == 2 and share % 8 == 0
    kept = [mine, repeat_table(channels)] if split_samples else []
    tall = (pairs, share, 2 * channels * channels)
    _, late = lax.optimization_barrier((grads, cotangent))
    linear, *weight_grad = call(
        functools.partial(local_kernel, len(kept)),
        [shape((channels, length_y, length_z), F32)] + [shape(tall, F32)] * (len(kept) // 2),
        [
            pltpu.VMEM((channels, length_y, length_z), BF16),
            pltpu.VMEM((16 * channels, 16 * channels), BF16),
            pltpu.SemaphoreType.DMA(()),
        ],
        16, 4 * 10**9, 5 * 10**6,
        in_hbm(late), pointwise_weight, *kept,
        in_specs=[hbm] + [pl.BlockSpec()] * (1 + len(kept)),
    )
    if split_samples:
        other = lax.ppermute(other, "dp", [(0, 1), (1, 0)])
        weight_grad = call(
            weight_kernel,
            shape(tall, F32),
            [pltpu.VMEM(tall, F32), pltpu.SemaphoreType.DMA((4,))],
            16, 2 * 10**9, 5 * 10**6,
            other, kept[1], *weight_grad,
            out_specs=hbm,
        )
    else:
        me = lax.axis_index("dp")
        modes = jnp.concatenate([mine[None], other.reshape(samples - 1, pairs, share, 128)])
        modes = jnp.roll(modes, me, 0)
        modes = lax.all_to_all(modes, "dp", split_axis=0, concat_axis=0, tiled=True)
        weight_grad = weight_terms(modes, channels)
    field_grad = call(
        inverse_kernel,
        shape((channels, length_y, length_z), BF16),
        [
            pltpu.VMEM((ROWS * (channels + 8), length_z), F32),
            pltpu.VMEM((channels, length_y, length_z), BF16),
            pltpu.SemaphoreType.DMA((channels // 8,)),
        ],
        16, 10**9, 4 * 10**6,
        returned.reshape(width_x * count, 128), linear, iz, iy,
        out_specs=hbm,
    )
    return field_grad.reshape(1, planes, channels, length_y, length_z), weight_grad


def solution(mesh):
    placed = (
        P("dp", "gx", None, None, None),
        P("dp", "gx", None, None, None),
        P("gx", None, None),
        P(),
    )
    return jax.shard_map(
        on_device,
        mesh=mesh,
        in_specs=placed,
        out_specs=(P("dp", "gx", None, None, None), P("gx", "dp", None)),
        check_vma=False,
    )
```
